32 devices in a mesh: groups: 2 (over y), occ: 4 (over z), vir: 2 (over x), rep: 2 (over core).
Axes of the slice: x: 2, y: 2, z: 4, core: 2. Of those that a mesh axis runs over, the one named last changes fastest.
Arguments:
- amps: float32 [8, 800, 800], P(('groups', 'occ'), ('vir', 'rep')), parts along dimension 0
- drive: float32 [8, 800, 800], P(('groups', 'occ'), ('vir', 'rep')), parts along dimension 0, may hold values from -6 to 6
- cycle_w: float32 [8, 8, 800, 800], P(('groups', 'occ'), None, None, ('vir', 'rep')), parts along dimension 0, may hold values from -0.21875 to 0.21875
- cycle_src: int32 [8, 8], P(('groups', 'occ')), parts along dimension 0, may hold values from 0 to 3
- cycle_count: int32 [8], P(('groups', 'occ')), parts along dimension 0, may hold values from 1 to 8, as said below
- ladder_src: int32 [8, 1], P(('groups', 'occ')), parts along dimension 0, may hold values from 0 to 3
- ladder_coef: float32 [8, 1], P(('groups', 'occ')), parts along dimension 0, may hold values from -1 to 1
- eps_vir: float32 [1600], P('groups'), parts along dimension 0, may hold values from 0.5 to 3
- pair_energy: float32 [8], P(('groups', 'occ')), parts along dimension 0, may hold values from -4 to -0.8
Outputs:
- residual: float32 [8, 800, 800], P(('groups', 'occ'), ('vir', 'rep')), parts along dimension 0
- update: float32 [8, 800, 800], P(('groups', 'occ'), ('vir', 'rep')), parts along dimension 0
The draws below stay inside these ranges and needn't reach their ends.
There are 2 independent parts, one for each index of `groups`. The reference program is written for one: setup_inputs(seed, part) draws one part's arguments, and reference() takes and returns one part's arrays. A program takes and returns all parts, laid end to end along the dimension named above; each array names one. Nothing has to cross between parts.
Inputs may be any that keep to these rules, and one draw needn't show every extreme that they name: `cycle_src`: pair indices. Only the first cycle_count[n] blocks of pair n count; some pair keeps all 8. `ladder_src`: pair indices.
All inputs are finite; a program needn't handle non-finite values.
Results may differ from the reference program's by a relative error of at most 0.00005.
Values sent between devices are 32-bit elements; how exact they have to be, the bound alone decides.
No kernel may reach another device: no remote copies, remote signals or barrier semaphores. Data moves between devices by JAX's collectives and lax.ppermute only.
A program may use at most 64 MiB of HBM per device.

```python
import math
import jax
import jax.numpy as jnp
from jax import lax

NV = 800
NRING = 8
NPAIR = 4
NLAD = 1


def draw_amps(key, part):
    key = jax.random.fold_in(key, 11)
    ramp = jnp.arange(NPAIR).astype(jnp.float32) / max(NPAIR - 1, 1)
    base = jax.random.normal(key, (NPAIR, NV, NV), jnp.float32)
    factor = 1.0 + 2.0 * ramp
    return base * factor[:, None, None]


def draw_cycle_count(key, part):
    key = jax.random.fold_in(key, 23)
    first, second, third = jax.random.split(key, 3)
    light = jax.random.randint(first, (NPAIR,), 1, NRING // 2 + 1)
    heavy = jax.random.randint(second, (NPAIR,), 0, 8) == 0
    counts = jnp.where(heavy, NRING, light)
    chosen = jax.random.randint(third, (), 0, NPAIR)
    return counts.at[chosen].set(NRING).astype(jnp.int32)


def set_ends(array, own_key, low, largest):
    index_at = [jax.random.randint(jax.random.fold_in(own_key, axis), (), 0, length) for axis, length in enumerate(array.shape)]
    main_axis = array.shape.index(max(array.shape))
    next_to = index_at[:main_axis] + [(index_at[main_axis] + 1) % array.shape[main_axis]] + index_at[main_axis + 1:]
    return array.at[tuple(index_at)].set(low).at[tuple(next_to)].set(largest)


def levels(rng, extent, shards, least, largest):
    level = 1.0
    for position, blocks in shards:
        steps = jax.random.uniform(jax.random.fold_in(jax.random.fold_in(rng, 6), position), (blocks,), jnp.float32, least / len(shards), largest / len(shards))
        level = level * jnp.repeat(jnp.exp(steps), extent[position] // blocks).reshape((-1,) + (1,) * (len(extent) - 1 - position))
    return level


def noise(stream_key, dims, scale, bound, cuts=(), held_as=jnp.bfloat16):
    result = jax.random.normal(stream_key, dims, jnp.float32) * scale
    if len(cuts) > 0:
        result = levels(stream_key, dims, cuts, -0.22, 0.18) * result
    return jnp.clip(result, min=-bound, max=bound).astype(held_as)


def setup_inputs(seed: int = 0, part: int = 0) -> dict:
    key_of = jax.random.split(jax.random.key(seed), 10)
    part_keys = jax.random.split(jax.random.fold_in(key_of[9], part), 10)
    return {
        "amps": draw_amps(jax.random.fold_in(jax.random.fold_in(key_of[9], part), 71), part),
        "drive": noise(part_keys[1], (NPAIR, NV, NV), 1.0, 6.0, ((0, 4), (1, 4)), jnp.float32),
        "cycle_w": noise(part_keys[2], (NPAIR, NRING, NV, NV), NV ** -0.5, 0.21875, ((0, 4), (3, 4)), jnp.float32),
        "cycle_src": set_ends(jax.random.randint(part_keys[3], (NPAIR, NRING), 0, NPAIR), jax.random.fold_in(part_keys[3], 1), 0, NPAIR - 1).astype(jnp.int32),
        "cycle_count": draw_cycle_count(jax.random.fold_in(jax.random.fold_in(key_of[9], part), 71), part),
        "ladder_src": set_ends(jax.random.randint(part_keys[5], (NPAIR, NLAD), 0, NPAIR), jax.random.fold_in(part_keys[5], 1), 0, NPAIR - 1).astype(jnp.int32),
        "ladder_coef": jnp.clip(jax.random.uniform(part_keys[6], (NPAIR, NLAD), jnp.float32, -1.0, 1.0) * levels(part_keys[6], (NPAIR, NLAD), ((0, 4),), -0.4, 0.0), -1.0, 1.0),
        "eps_vir": jnp.clip(jax.random.uniform(part_keys[7], (NV,), jnp.float32, 0.5, 3.0), 0.5, 3.0),
        "pair_energy": jnp.clip(-4.0 + 3.2 * jax.random.uniform(part_keys[8], (NPAIR,), jnp.float32) ** levels(part_keys[8], (NPAIR,), ((0, 4),), -0.2, 0.2), -4.0, -0.8),
    }


clip_level = 0.5

def reference(amps, drive, cycle_w, cycle_src, cycle_count, ladder_src, ladder_coef, eps_vir, pair_energy):
    largest_value = lax.Precision.HIGHEST
    live = (jnp.arange(NRING)[None, :] < cycle_count[:, None]).astype(jnp.float32)

    def cycle_one(packed):
        pair_block_list, sources, retain_mask = packed
        selected_rows = amps[sources]
        return jnp.einsum('rkd,rdp->kp', pair_block_list * retain_mask[:, None, None], selected_rows, precision=largest_value)
    cycle = lax.map(cycle_one, (cycle_w, cycle_src, live))
    indicator_matrix = (ladder_src[:, :, None] == jnp.arange(NPAIR)[None, None, :]).astype(jnp.float32)
    ladder_matrix = lax.optimization_barrier(jnp.sum(ladder_coef[:, :, None] * indicator_matrix, axis=1))
    ladder = jnp.einsum('nm,mab->nab', ladder_matrix, amps, precision=largest_value)
    denom = eps_vir[None, :, None] + eps_vir[None, None, :] - pair_energy[:, None, None]
    residual = drive + cycle + ladder - denom * amps
    total = jnp.sum(residual * residual)
    scale = jnp.minimum(1.0, clip_level * NV * math.sqrt(NPAIR) / jnp.sqrt(total))
    update = scale * residual / denom
    return (residual, update)
```

```python
import functools
import math

import jax
import jax.numpy as jnp
from jax import lax
from jax.experimental import pallas as pl
from jax.experimental.pallas import tpu as pltpu
from jax.sharding import PartitionSpec as P

clip_level = 0.5
LANES = 128
SMEM = pl.BlockSpec(memory_space=pltpu.SMEM)
SWAP = [(0, 1), (1, 0)]
ENDS = [(0, 1), (1, 0), (2, 3), (3, 2)]
MIDDLE = [(1, 2), (2, 1)]
OUTWARD = [(1, 0), (2, 3)]
ACROSS = [(0, 2), (2, 0), (1, 3), (3, 1)]


def limit(n):
    return pltpu.CompilerParams(vmem_limit_bytes=n << 20)


class Chunk:
    def __init__(self, rows, width, first, count, rest):
        self.rows, self.first, self.count = rows, first, count
        self.rest = width % LANES if rest else 0
        self.at = width - self.rest
        self.group = -(-rows // 32) * 8
        self.length = rows * count + (self.group if self.rest else 0)
        self.width = LANES * count + self.rest

    def take(self, ref):
        parts = [ref[:, self.first * LANES : (self.first + self.count) * LANES]]
        if self.rest:
            parts.append(ref[:, self.at : self.at + self.rest])
        return jnp.concatenate(parts, axis=1) if len(parts) > 1 else parts[0]

    def put(self, ref, value):
        span = LANES * self.count
        ref[:, self.first * LANES : self.first * LANES + span] = value[:, :span]
        if self.rest:
            ref[:, self.at : self.at + self.rest] = value[:, span:]

    def load(self, read):
        parts = [read(t * self.rows, self.rows) for t in range(self.count)]
        if self.rest:
            packed = read(self.count * self.rows, self.group)
            rest = [packed[:, g * self.rest : (g + 1) * self.rest] for g in range(4)]
            parts.append(jnp.concatenate(rest, axis=0)[: self.rows])
        return jnp.concatenate(parts, axis=1)

    def store(self, write, value):
        for t in range(self.count):
            write(t * self.rows, self.rows, value[:, t * LANES : (t + 1) * LANES])
        if self.rest:
            rest = value[:, self.count * LANES :]
            short = 4 * self.group - self.rows
            rest = jnp.concatenate([rest, jnp.zeros((short, self.rest), rest.dtype)], axis=0)
            groups = [rest[g * self.group : (g + 1) * self.group] for g in range(4)]
            write(self.count * self.rows, self.group, jnp.concatenate(groups, axis=1))


def reader(ref, lead=()):
    return lambda start, size: ref[(*lead, pl.ds(start, size), slice(None))]


def writer(ref, lead=()):
    def write(start, size, value):
        ref[(*lead, pl.ds(start, size), slice(None))] = value

    return write


def split(value):
    high = value.astype(jnp.bfloat16)
    return high, (value - high.astype(jnp.float32)).astype(jnp.bfloat16)


def product(high, low, x_high, x_low):
    dot = functools.partial(jnp.dot, preferred_element_type=jnp.float32)
    return dot(high, x_high) + (dot(low, x_high) + dot(high, x_low))


def pack(amps, chunks):
    def kernel(amps_ref, *outs):
        for chunk, out in zip(chunks, outs, strict=True):
            chunk.store(writer(out), chunk.take(amps_ref))

    return pl.pallas_call(
        kernel,
        out_shape=[jax.ShapeDtypeStruct((c.length, LANES), jnp.float32) for c in chunks],
        name="pack",
    )(amps)


def sum_by_source(cycle_w, cycle_src, cycle_count, npair, blocks):
    nring, height, depth = cycle_w.shape
    rows = height // blocks

    def kernel(src_ref, count_ref, w_ref, high_ref, low_ref, total):
        total[...] = jnp.zeros_like(total)
        for s in range(nring):

            @pl.when(s < count_ref[0])
            def _():
                source = src_ref[0, s]
                total[source] = total[source] + w_ref[s]

        for m in range(npair):
            high, low = split(total[m])
            high_ref[m, 0] = high
            low_ref[m, 0] = low

    block = pl.BlockSpec((npair, 1, rows, depth), lambda j: (0, j, 0, 0))
    shape = jax.ShapeDtypeStruct((npair, blocks, rows, depth), jnp.bfloat16)
    return pl.pallas_call(
        kernel,
        grid=(blocks,),
        in_specs=[SMEM, SMEM, pl.BlockSpec((nring, rows, depth), lambda j: (0, j, 0))],
        out_specs=[block, block],
        out_shape=[shape, shape],
        scratch_shapes=[pltpu.VMEM((npair, rows, depth), jnp.float32)],
        compiler_params=limit(32),
        name="sum_by_source",
    )(cycle_src, cycle_count, cycle_w)


def ladder_weight(source, lad_src, lad_coef):
    weight = jnp.float32(0)
    for entry in range(lad_src.shape[1]):
        weight = weight + jnp.where(lad_src[0, entry] == source, lad_coef[0, entry], 0.0)
    return weight


def first_stage(chunk, meta, lad_src, lad_coef, energy, weights, own, near, drive, eps_row, eps_col):
    high, low = weights
    _, blocks, rows, depth = high.shape

    def kernel(meta, lad_src, lad_coef, energy, h0, l0, h1, l1, own, near, drive, eps_row, eps_col, away, keep, xs):
        j = pl.program_id(0)

        @pl.when(j == 0)
        def _():
            for i, ref in enumerate((own, near)):
                xs[2 * i], xs[2 * i + 1] = split(chunk.load(reader(ref)))

        value = product(h0[0, 0], l0[0, 0], xs[0], xs[1]) + product(h1[0, 0], l1[0, 0], xs[2], xs[3])

        @pl.when(j < 2)
        def _():
            chunk.store(writer(away, (0,)), value)

        @pl.when(j == 2)
        def _():
            chunk.store(writer(keep, (0,)), value)

        @pl.when(j == 3)
        def _():
            mine = chunk.load(reader(own))
            denom = eps_col[...] + chunk.take(eps_row) - energy[0]
            base = chunk.take(drive) - denom * mine
            base = base + ladder_weight(meta[0], lad_src, lad_coef) * mine
            base = base + ladder_weight(meta[1], lad_src, lad_coef) * chunk.load(reader(near))
            chunk.store(writer(keep, (0,)), value + base)

    def weight_block(k):
        return pl.BlockSpec((1, 1, rows, depth), lambda j, meta: (meta[k], meta[5 + j], 0, 0))

    def whole(a):
        return pl.BlockSpec(a.shape, lambda j, meta: (0,) * a.ndim)

    out = jax.ShapeDtypeStruct((2, chunk.length, LANES), jnp.float32)
    return pl.pallas_call(
        kernel,
        grid_spec=pltpu.PrefetchScalarGridSpec(
            num_scalar_prefetch=1,
            grid=(blocks,),
            in_specs=[SMEM, SMEM, SMEM]
            + [weight_block(0), weight_block(0), weight_block(1), weight_block(1)]
            + [whole(a) for a in (own, near, drive, eps_row, eps_col)],
            out_specs=[
                pl.BlockSpec((1, chunk.length, LANES), lambda j, meta: (jnp.minimum(j, 1), 0, 0)),
                pl.BlockSpec((1, chunk.length, LANES), lambda j, meta: (jnp.maximum(j - 2, 0), 0, 0)),
            ],
            scratch_shapes=[pltpu.VMEM((4, rows, chunk.width), jnp.bfloat16)],
        ),
        out_shape=[out, out],
        compiler_params=limit(32),
        name="first_stage",
    )(meta, lad_src, lad_coef, energy, high, low, high, low, own, near, drive, eps_row, eps_col)


def next_stage(chunk, k, meta, lad_src, lad_coef, weights, inner, outer, away, keep):
    high, low = weights
    _, blocks, rows, depth = high.shape

    def kernel(meta, lad_src, lad_coef, h, l, inner, outer, away_in, keep_in, away, keep, xs, x):
        j = pl.program_id(0)

        @pl.when(j == 0)
        def _():
            @pl.when(meta[4] == 1)
            def _():
                x[...] = chunk.load(reader(inner))

            @pl.when(meta[4] == 0)
            def _():
                x[...] = chunk.load(reader(outer))

            xs[0], xs[1] = split(x[...])

        value = product(h[0, 0], l[0, 0], xs[0], xs[1])

        @pl.when(j < 2)
        def _():
            chunk.store(writer(away, (0,)), value + chunk.load(reader(away_in, (0,))))

        @pl.when(j >= 2)
        def _():
            weight = jnp.where(j == 3, ladder_weight(meta[k], lad_src, lad_coef), 0.0)
            chunk.store(writer(keep, (0,)), value + weight * x[...] + chunk.load(reader(keep_in, (0,))))

    def whole(a):
        return pl.BlockSpec(a.shape, lambda j, meta: (0,) * a.ndim)

    weight_block = pl.BlockSpec((1, 1, rows, depth), lambda j, meta: (meta[k], meta[5 + j], 0, 0))
    sums = [
        pl.BlockSpec((1, chunk.length, LANES), lambda j, meta: (jnp.minimum(j, 1), 0, 0)),
        pl.BlockSpec((1, chunk.length, LANES), lambda j, meta: (jnp.maximum(j - 2, 0), 0, 0)),
    ]
    out = jax.ShapeDtypeStruct((2, chunk.length, LANES), jnp.float32)
    return pl.pallas_call(
        kernel,
        grid_spec=pltpu.PrefetchScalarGridSpec(
            num_scalar_prefetch=1,
            grid=(blocks,),
            in_specs=[SMEM, SMEM, weight_block, weight_block, whole(inner), whole(outer), *sums],
            out_specs=sums,
            scratch_shapes=[
                pltpu.VMEM((2, rows, chunk.width), jnp.bfloat16),
                pltpu.VMEM((rows, chunk.width), jnp.float32),
            ],
        ),
        out_shape=[out, out],
        compiler_params=limit(32),
        name="next_stage",
    )(meta, lad_src, lad_coef, high, low, inner, outer, away, keep)


def finish(chunks, pieces, shape):
    def kernel(*refs):
        *ins, out, total_ref = refs
        total = jnp.float32(0)
        for i, chunk in enumerate(chunks):
            keep, got, far = ins[3 * i : 3 * i + 3]
            value = chunk.load(reader(keep, (1,))) + chunk.load(reader(got, (1,))) + chunk.load(reader(far))
            chunk.put(out, value)
            total = total + jnp.sum(value * value)
        total_ref[...] = jnp.broadcast_to(total, total_ref.shape)

    return pl.pallas_call(
        kernel,
        out_shape=[
            jax.ShapeDtypeStruct(shape, jnp.float32),
            jax.ShapeDtypeStruct((8, LANES), jnp.float32),
        ],
        compiler_params=limit(32),
        name="finish",
    )(*pieces)


def jacobi(residual, total, energy, eps_row, eps_col, bound):
    def kernel(energy, residual, total, eps_row, eps_col, out):
        scale = jnp.minimum(1.0, bound / jnp.sqrt(total[0:1, 0:1]))
        denom = eps_col[...] + eps_row[...] - energy[0]
        out[...] = scale * residual[...] / denom

    vmem = pl.BlockSpec(memory_space=pltpu.VMEM)
    return pl.pallas_call(
        kernel,
        in_specs=[SMEM, vmem, vmem, vmem, vmem],
        out_shape=jax.ShapeDtypeStruct(residual.shape, jnp.float32),
        compiler_params=limit(32),
        name="jacobi",
    )(energy, residual, total, eps_row, eps_col)


def chain_body(amps, drive, cycle_w, cycle_src, cycle_count, ladder_src, ladder_coef, eps_vir, pair_energy):
    _, rows, width = amps.shape
    npair, blocks = lax.axis_size("occ"), width // rows
    place, chip, core = lax.axis_index("occ"), lax.axis_index("vir"), lax.axis_index("rep")
    low_half = place < 2
    order = [
        place,
        place ^ 1,
        jnp.where(low_half, 2, 1),
        jnp.where(low_half, 3, 0),
        ((place == 1) | (place == 2)).astype(jnp.int32),
        2 * (1 - chip) + (1 - core),
        2 * chip + (1 - core),
        2 * (1 - chip) + core,
        2 * chip + core,
    ]
    meta = jnp.stack([jnp.asarray(v, jnp.int32) for v in order])
    eps_row = eps_vir.reshape(1, width)
    eps_col = lax.dynamic_slice_in_dim(eps_vir, (2 * chip + core) * rows, rows).reshape(rows, 1)

    tiles = width // LANES
    half = tiles // 2
    chunks = [Chunk(rows, width, 0, half, True), Chunk(rows, width, half, tiles - half, False)]
    own = pack(amps[0], chunks)
    weights = sum_by_source(cycle_w[0], cycle_src, cycle_count, npair, blocks)

    send = functools.partial(lax.ppermute, axis_name="occ")
    ends = [send(x, perm=ENDS) for x in own]
    middle = [send(x, perm=MIDDLE) for x in own]
    second = [send(x, perm=OUTWARD) for x in middle]
    across = [send(x, perm=MIDDLE) for x in ends]
    third = [send(x, perm=OUTWARD) for x in across]

    pieces = []
    for i, chunk in enumerate(chunks):
        sums = first_stage(
            chunk, meta, ladder_src, ladder_coef, pair_energy, weights,
            own[i], ends[i], drive[0], eps_row, eps_col,
        )
        sums = next_stage(chunk, 2, meta, ladder_src, ladder_coef, weights, middle[i], second[i], *sums)
        away, keep = next_stage(chunk, 3, meta, ladder_src, ladder_coef, weights, across[i], third[i], *sums)
        got = lax.ppermute(away, "rep", SWAP)
        far = lax.ppermute(keep[0] + got[0], "vir", SWAP)
        pieces += [keep, got, far]
    residual, total = finish(chunks, pieces, (rows, width))
    for axis, perm in (("rep", SWAP), ("vir", SWAP), ("occ", ENDS), ("occ", ACROSS)):
        total = total + lax.ppermute(total, axis, perm)
    update = jacobi(residual, total, pair_energy, eps_row, eps_col, clip_level * width * math.sqrt(npair))
    return residual[None], update[None]


def any_body(amps, drive, cycle_w, cycle_src, cycle_count, ladder_src, ladder_coef, eps_vir, pair_energy):
    largest_value = lax.Precision.HIGHEST
    pairs_per_unit, rows, width = amps.shape
    nring = cycle_w.shape[1]
    npair = pairs_per_unit * lax.axis_size("occ")
    all_rows = lax.all_gather(amps, "occ", axis=0, tiled=True)
    ladder = jnp.sum(ladder_coef[:, :, None, None] * all_rows[ladder_src], axis=1)
    selected_rows = jnp.take(all_rows, cycle_src.reshape(-1), axis=0).reshape(
        pairs_per_unit, nring, rows, width
    )
    live = (jnp.arange(nring)[None, :] < cycle_count[:, None]).astype(jnp.float32)
    partial_value = jnp.einsum(
        "ptac,ptcb->pab", cycle_w * live[:, :, None, None], selected_rows, precision=largest_value
    )
    cycle = lax.psum_scatter(partial_value, ("vir", "rep"), scatter_dimension=1, tiled=True)
    first_row = lax.axis_index(("vir", "rep")) * rows
    eps_rows = lax.dynamic_slice_in_dim(eps_vir, first_row, rows)
    denom = eps_rows[None, :, None] + eps_vir[None, None, :] - pair_energy[:, None, None]
    residual = drive + cycle + ladder - denom * amps
    total = lax.psum(jnp.sum(residual * residual), ("occ", "vir", "rep"))
    scale = jnp.minimum(1.0, clip_level * width * math.sqrt(npair) / jnp.sqrt(total))
    return residual, scale * residual / denom


def body(*args):
    amps, cycle_w = args[0], args[2]
    pairs_per_unit, rows, width = amps.shape
    chain = (
        pairs_per_unit == 1
        and (lax.axis_size("occ"), lax.axis_size("vir"), lax.axis_size("rep")) == (4, 2, 2)
        and cycle_w.shape[1] >= 4
        and rows % 8 == 0
        and width % LANES == LANES // 4
        and width >= 2 * LANES
    )
    return (chain_body if chain else any_body)(*args)


def solution(mesh):
    in_specs = (
        P(("groups", "occ"), ("vir", "rep"), None),
        P(("groups", "occ"), ("vir", "rep"), None),
        P(("groups", "occ"), None, None, ("vir", "rep")),
        P(("groups", "occ"), None),
        P(("groups", "occ")),
        P(("groups", "occ"), None),
        P(("groups", "occ"), None),
        P("groups"),
        P(("groups", "occ")),
    )
    out_specs = (
        P(("groups", "occ"), ("vir", "rep"), None),
        P(("groups", "occ"), ("vir", "rep"), None),
    )
    return jax.shard_map(body, mesh=mesh, in_specs=in_specs, out_specs=out_specs, check_vma=False)
```

```python
import functools
import math

import jax
import jax.numpy as jnp
from jax import lax
from jax.experimental import pallas as pl
from jax.experimental.pallas import tpu as pltpu
from jax.sharding import PartitionSpec as P

clip_level = 0.5
LANES = 128
SMEM = pl.BlockSpec(memory_space=pltpu.SMEM)
VMEM = pl.BlockSpec(memory_space=pltpu.VMEM)
HBM = pl.BlockSpec(memory_space=pl.ANY)
SWAP = [(0, 1), (1, 0)]
NEAR = [(0, 1), (1, 0), (2, 3), (3, 2)]
FAR = [(0, 2), (2, 0), (1, 3), (3, 1)]
VMEM_MIB = 20
TILES_FIRST = 2
MERGE = True
FORCE = True


def limit(n):
    return pltpu.CompilerParams(vmem_limit_bytes=n << 20)


class Chunk:
    def __init__(self, rows, width, first, count, rest, start):
        self.rows, self.first, self.count, self.start = rows, first, count, start
        self.rest = width % LANES if rest else 0
        self.at = width - self.rest
        self.group = -(-rows // 32) * 8
        self.length = rows * count + (self.group if self.rest else 0)
        self.width = LANES * count + self.rest

    def take(self, ref):
        parts = [ref[:, self.first * LANES : (self.first + self.count) * LANES]]
        if self.rest:
            parts.append(ref[:, self.at : self.at + self.rest])
        return jnp.concatenate(parts, axis=1) if len(parts) > 1 else parts[0]

    def put(self, ref, value):
        span = LANES * self.count
        ref[:, self.first * LANES : self.first * LANES + span] = value[:, :span]
        if self.rest:
            ref[:, self.at : self.at + self.rest] = value[:, span:]

    def load(self, read):
        parts = [read(t * self.rows, self.rows) for t in range(self.count)]
        if self.rest:
            packed = read(self.count * self.rows, self.group)
            rest = [packed[:, g * self.rest : (g + 1) * self.rest] for g in range(4)]
            parts.append(jnp.concatenate(rest, axis=0)[: self.rows])
        return jnp.concatenate(parts, axis=1)

    def store(self, write, value):
        for t in range(self.count):
            write(t * self.rows, self.rows, value[:, t * LANES : (t + 1) * LANES])
        if self.rest:
            rest = value[:, self.count * LANES :]
            short = 4 * self.group - self.rows
            rest = jnp.concatenate([rest, jnp.zeros((short, self.rest), rest.dtype)], axis=0)
            groups = [rest[g * self.group : (g + 1) * self.group] for g in range(4)]
            write(self.count * self.rows, self.group, jnp.concatenate(groups, axis=1))


def reader(ref, lead=(), skip=0):
    return lambda start, size: ref[(*lead, pl.ds(skip + start, size), slice(None))]


def writer(ref, lead=(), skip=0):
    def write(start, size, value):
        ref[(*lead, pl.ds(skip + start, size), slice(None))] = value

    return write


def split(value):
    high = value.astype(jnp.bfloat16)
    return high, (value - high.astype(jnp.float32)).astype(jnp.bfloat16)


def product(high, low, x_high, x_low):
    dot = functools.partial(jnp.dot, preferred_element_type=jnp.float32)
    return dot(high, x_high) + (dot(low, x_high) + dot(high, x_low))


def pack(amps, chunks):
    def kernel(amps_ref, out):
        for chunk in chunks:
            chunk.store(writer(out, skip=chunk.start), chunk.take(amps_ref))

    length = sum(chunk.length for chunk in chunks)
    return pl.pallas_call(
        kernel,
        in_specs=[VMEM],
        out_specs=VMEM,
        out_shape=jax.ShapeDtypeStruct((length, LANES), jnp.float32),
        name="pack",
    )(amps)


def sum_by_source(meta, cycle_w, cycle_src, cycle_count, npair, blocks):
    nring, depth, height = cycle_w.shape
    rows = height // blocks
    tall, deep = -(-height // LANES) * LANES, -(-depth // LANES) * LANES

    def kernel(meta, src, count, w_ref, high_ref, low_ref, total, turned, ordered):
        s = pl.program_id(0)

        @pl.when(s == 0)
        def _():
            total[...] = jnp.zeros_like(total)

        @pl.when(s < count[0])
        def _():
            source = src[s]
            total[source, :depth, :height] = total[source, :depth, :height] + w_ref[0]

        @pl.when(s == nring - 1)
        def _():
            for m in range(npair):
                turned[...] = total[m].T
                for j in range(blocks):
                    start = pl.multiple_of(meta[4 + j] * rows, 8)
                    ordered[j * rows : (j + 1) * rows] = turned[pl.ds(start, rows), :depth]
                for h in range(2):
                    high_ref[m, h], low_ref[m, h] = split(ordered[h * height // 2 : (h + 1) * height // 2])

    block = pl.BlockSpec((npair, 2, height // 2, depth), lambda s, *_: (0, 0, 0, 0))
    shape = jax.ShapeDtypeStruct((npair, 2, height // 2, depth), jnp.bfloat16)
    return pl.pallas_call(
        kernel,
        grid_spec=pltpu.PrefetchScalarGridSpec(
            num_scalar_prefetch=3,
            grid=(nring,),
            in_specs=[
                pl.BlockSpec(
                    (1, depth, height), lambda s, meta, src, count: (jnp.minimum(s, count[0] - 1), 0, 0)
                )
            ],
            out_specs=[block, block],
            scratch_shapes=[
                pltpu.VMEM((npair, deep, tall), jnp.float32),
                pltpu.VMEM((tall, deep), jnp.float32),
                pltpu.VMEM((height, depth), jnp.float32),
            ],
        ),
        out_shape=[shape, shape],
        compiler_params=limit(VMEM_MIB),
        name="sum_by_source",
    )(meta, cycle_src.reshape(-1), cycle_count, cycle_w)


def ladder_weight(source, lad_src, lad_coef):
    weight = jnp.float32(0)
    for entry in range(lad_src.shape[1]):
        weight = weight + jnp.where(lad_src[0, entry] == source, lad_coef[0, entry], 0.0)
    return weight


def own_products(chunks, meta, lad_src, lad_coef, energy, weights, amps, drive, eps_row, eps_col):
    high, low = weights
    _, _, height, _ = high.shape
    rows = drive.shape[0]

    def kernel(meta, lad_src, lad_coef, energy, high, low, amps, drive, eps_row, eps_col, inverse, *outs):
        denom = eps_col[...] + eps_row[...] - energy[0]
        inverse[...] = 1.0 / denom
        weight = ladder_weight(meta[0], lad_src, lad_coef)
        for chunk, out in zip(chunks, outs, strict=True):
            mine = chunk.load(reader(amps, skip=chunk.start))
            x_high, x_low = split(mine)
            for h in range(2):
                out[h] = product(high[meta[0], h], low[meta[0], h], x_high, x_low)
            denom = eps_col[...] + chunk.take(eps_row) - energy[0]
            base = chunk.take(drive) - denom * mine + weight * mine
            out[1, height - rows :] = out[1, height - rows :] + base

    return pl.pallas_call(
        kernel,
        in_specs=[SMEM] * 4 + [VMEM] * 6,
        out_specs=[VMEM] * (1 + len(chunks)),
        out_shape=[jax.ShapeDtypeStruct(drive.shape, jnp.float32)]
        + [jax.ShapeDtypeStruct((2, height, c.width), jnp.float32) for c in chunks],
        compiler_params=limit(VMEM_MIB),
        name="own_products",
    )(meta, lad_src, lad_coef, energy, high, low, amps, drive, eps_row, eps_col)


def add_products(chunks, ks, meta, lad_src, lad_coef, weights, packed, sums):
    high, low = weights
    _, _, height, _ = high.shape
    rows = chunks[0].rows
    n = len(ks)

    def kernel(meta, lad_src, lad_coef, high, low, *refs):
        packed, refs = refs[:n], refs[n:]
        for c, chunk in enumerate(chunks):
            sums, out = refs[c :: len(chunks)]
            amps = [chunk.load(reader(ref, skip=chunk.start)) for ref in packed]
            parts = [split(x) for x in amps]
            for h in range(2):
                value = sums[h]
                for k, (x_high, x_low) in zip(ks, parts, strict=True):
                    value = value + product(high[meta[k], h], low[meta[k], h], x_high, x_low)
                out[h] = value
            value = out[1, height - rows :]
            for k, x in zip(ks, amps, strict=True):
                value = value + ladder_weight(meta[k], lad_src, lad_coef) * x
            out[1, height - rows :] = value

    return pl.pallas_call(
        kernel,
        in_specs=[SMEM] * 3 + [VMEM] * (2 + n + len(chunks)),
        out_specs=[VMEM] * len(chunks),
        out_shape=[jax.ShapeDtypeStruct(s.shape, jnp.float32) for s in sums],
        compiler_params=limit(VMEM_MIB),
        name="add_products",
    )(meta, lad_src, lad_coef, high, low, *packed, *sums)


def last_product(chunk, meta, lad_src, lad_coef, weights, amps, sums):
    high, low = weights
    npair, _, height, _ = high.shape
    rows = chunk.rows

    def kernel(meta, lad_src, lad_coef, high, low, amps, sums, *outs):
        k = meta[npair - 1]
        x = chunk.load(reader(amps))
        x_high, x_low = split(x)
        for h in range(2):
            value = sums[h] + product(high[k, h], low[k, h], x_high, x_low)
            for i in range(2):
                part = value[i * rows : (i + 1) * rows]
                if h and i:
                    part = part + ladder_weight(k, lad_src, lad_coef) * x
                chunk.store(writer(outs[2 * h + i]), part)

    return pl.pallas_call(
        kernel,
        in_specs=[SMEM] * 3 + [VMEM] * 4,
        out_specs=[VMEM] * 4,
        out_shape=[jax.ShapeDtypeStruct((chunk.length, LANES), jnp.float32)] * 4,
        compiler_params=limit(VMEM_MIB),
        name="last_product",
    )(meta, lad_src, lad_coef, high, low, amps, sums)


def finish(chunks, done, pieces, shape, copies):
    def kernel(*refs):
        *refs, out, total_ref = refs
        total = jnp.zeros((1, LANES), jnp.float32)
        for i, chunk in enumerate(chunks):
            parts = refs[i : i + 1] if i < len(done) else refs[len(done) + 3 * (i - len(done)) :][:3]
            value = sum(chunk.load(reader(ref)) for ref in parts)
            chunk.put(out, value)
            total = total + jnp.sum(value * value)
        total_ref[...] = jnp.broadcast_to(total, total_ref.shape)

    refs = [*done, *pieces]
    return pl.pallas_call(
        kernel,
        in_specs=[VMEM] * len(refs),
        out_specs=[VMEM, VMEM],
        out_shape=[
            jax.ShapeDtypeStruct(shape, jnp.float32),
            jax.ShapeDtypeStruct((copies, 8, LANES), jnp.float32),
        ],
        compiler_params=limit(VMEM_MIB),
        name="finish",
    )(*refs)


def jacobi(residual, total, inverse, bound):
    def kernel(residual, total, inverse, residual_out, update_out, update, sems):
        whole = pltpu.make_async_copy(residual, residual_out, sems.at[0])
        whole.start()
        scale = jnp.minimum(1.0, bound / jnp.sqrt(jnp.sum(total[...], axis=0)[0:1, 0:1]))
        update[...] = (scale * residual[...]) * inverse[...]
        moved = pltpu.make_async_copy(update, update_out, sems.at[1])
        moved.start()
        whole.wait()
        moved.wait()

    shape = jax.ShapeDtypeStruct(residual.shape, jnp.float32)
    return pl.pallas_call(
        kernel,
        in_specs=[VMEM, VMEM, VMEM],
        out_specs=[HBM, HBM],
        out_shape=[shape, shape],
        scratch_shapes=[pltpu.VMEM(residual.shape, jnp.float32), pltpu.SemaphoreType.DMA((2,))],
        compiler_params=limit(VMEM_MIB),
        name="jacobi",
    )(residual, total, inverse)


def chain_body(amps, drive, cycle_w, cycle_src, cycle_count, ladder_src, ladder_coef, eps_vir, pair_energy):
    _, rows, width = amps.shape
    npair, blocks = lax.axis_size("occ"), width // rows
    place, chip, core = lax.axis_index("occ"), lax.axis_index("vir"), lax.axis_index("rep")
    order = [
        place,
        place ^ 1,
        place ^ 2,
        place ^ 3,
        2 * (1 - chip) + (1 - core),
        2 * chip + (1 - core),
        2 * (1 - chip) + core,
        2 * chip + core,
    ]
    meta = jnp.stack([jnp.asarray(v, jnp.int32) for v in order])
    eps_row = eps_vir.reshape(1, width)
    eps_col = lax.dynamic_slice_in_dim(eps_vir, (2 * chip + core) * rows, rows).reshape(rows, 1)

    tiles = width // LANES
    half = TILES_FIRST
    first = Chunk(rows, width, 0, half, True, 0)
    chunks = [first, Chunk(rows, width, half, tiles - half, False, first.length)]
    own = pack(amps[0], chunks)
    far_amps = lax.ppermute(own, "occ", FAR)
    near_amps = lax.ppermute(own, "occ", NEAR)
    weights = sum_by_source(meta, jnp.swapaxes(cycle_w[0], 1, 2), cycle_src, cycle_count, npair, blocks)
    inverse, *sums = own_products(
        chunks, meta, ladder_src, ladder_coef, pair_energy, weights, own, drive[0], eps_row, eps_col
    )
    far_amps, sums = lax.optimization_barrier((far_amps, sums))
    last_amps = [lax.ppermute(far_amps[c.start : c.start + c.length], "occ", NEAR) for c in chunks]
    if MERGE:
        sums = add_products(
            chunks, (1, 2), meta, ladder_src, ladder_coef, weights, (near_amps, far_amps), sums
        )

    done, pieces = [], []
    for i, chunk in enumerate(chunks):
        if not MERGE:
            sums[i] = add_products(
                [chunk], (1, 2), meta, ladder_src, ladder_coef, weights, (near_amps, far_amps), [sums[i]]
            )[0]
        away = last_product(chunk, meta, ladder_src, ladder_coef, weights, last_amps[i], sums[i])
        away, keep = away[:2], away[2:]
        got = [lax.ppermute(x, "rep", SWAP) for x in away]
        for_far = keep[0] + got[0]
        if i and FORCE:
            done, for_far = lax.optimization_barrier((done, for_far))
        far = lax.ppermute(for_far, "vir", SWAP)
        if i < len(chunks) - 1 and FORCE:
            done.append(keep[1] + got[1] + far)
        else:
            pieces += [keep[1], got[1], far]
    residual, total = finish(chunks, done, pieces, (rows, width), npair * blocks)
    total = lax.all_to_all(total, ("occ", "vir", "rep"), split_axis=0, concat_axis=0, tiled=True)
    residual, update = jacobi(residual, total, inverse, clip_level * width * math.sqrt(npair))
    return residual[None], update[None]


def any_body(amps, drive, cycle_w, cycle_src, cycle_count, ladder_src, ladder_coef, eps_vir, pair_energy):
    largest_value = lax.Precision.HIGHEST
    pairs_per_unit, rows, width = amps.shape
    nring = cycle_w.shape[1]
    npair = pairs_per_unit * lax.axis_size("occ")
    all_rows = lax.all_gather(amps, "occ", axis=0, tiled=True)
    ladder = jnp.sum(ladder_coef[:, :, None, None] * all_rows[ladder_src], axis=1)
    selected_rows = jnp.take(all_rows, cycle_src.reshape(-1), axis=0).reshape(
        pairs_per_unit, nring, rows, width
    )
    live = (jnp.arange(nring)[None, :] < cycle_count[:, None]).astype(jnp.float32)
    partial_value = jnp.einsum(
        "ptac,ptcb->pab", cycle_w * live[:, :, None, None], selected_rows, precision=largest_value
    )
    cycle = lax.psum_scatter(partial_value, ("vir", "rep"), scatter_dimension=1, tiled=True)
    first_row = lax.axis_index(("vir", "rep")) * rows
    eps_rows = lax.dynamic_slice_in_dim(eps_vir, first_row, rows)
    denom = eps_rows[None, :, None] + eps_vir[None, None, :] - pair_energy[:, None, None]
    residual = drive + cycle + ladder - denom * amps
    total = lax.psum(jnp.sum(residual * residual), ("occ", "vir", "rep"))
    scale = jnp.minimum(1.0, clip_level * width * math.sqrt(npair) / jnp.sqrt(total))
    return residual, scale * residual / denom


def body(*args):
    amps, cycle_w = args[0], args[2]
    pairs_per_unit, rows, width = amps.shape
    chain = (
        pairs_per_unit == 1
        and (lax.axis_size("occ"), lax.axis_size("vir"), lax.axis_size("rep")) == (4, 2, 2)
        and cycle_w.shape[1] >= 4
        and rows % 8 == 0
        and width % LANES == LANES // 4
        and width >= 2 * LANES
    )
    return (chain_body if chain else any_body)(*args)


def solution(mesh):
    in_specs = (
        P(("groups", "occ"), ("vir", "rep"), None),
        P(("groups", "occ"), ("vir", "rep"), None),
        P(("groups", "occ"), None, None, ("vir", "rep")),
        P(("groups", "occ"), None),
        P(("groups", "occ")),
        P(("groups", "occ"), None),
        P(("groups", "occ"), None),
        P("groups"),
        P(("groups", "occ")),
    )
    out_specs = (
        P(("groups", "occ"), ("vir", "rep"), None),
        P(("groups", "occ"), ("vir", "rep"), None),
    )
    return jax.shard_map(body, mesh=mesh, in_specs=in_specs, out_specs=out_specs, check_vma=False)
```

```python
import functools
import math

import jax
import jax.numpy as jnp
from jax import lax
from jax.experimental import pallas as pl
from jax.experimental.pallas import tpu as pltpu
from jax.sharding import PartitionSpec as P

clip_level = 0.5
LANES = 128
SMEM = pl.BlockSpec(memory_space=pltpu.SMEM)
VMEM = pl.BlockSpec(memory_space=pltpu.VMEM)
HBM = pl.BlockSpec(memory_space=pl.ANY)
SWAP = [(0, 1), (1, 0)]
NEAR = [(0, 1), (1, 0), (2, 3), (3, 2)]
FAR = [(0, 2), (2, 0), (1, 3), (3, 1)]
VMEM_MIB = 20
FIRST_TILES = 2


def limit(n):
    return pltpu.CompilerParams(vmem_limit_bytes=n << 20)


class Chunk:
    def __init__(self, rows, width, first, count, rest, start):
        self.rows, self.first, self.count, self.start = rows, first, count, start
        self.rest = width % LANES if rest else 0
        self.at = width - self.rest
        self.group = -(-rows // 32) * 8
        self.length = rows * count + (self.group if self.rest else 0)
        self.width = LANES * count + self.rest

    def take(self, ref):
        parts = [ref[:, self.first * LANES : (self.first + self.count) * LANES]]
        if self.rest:
            parts.append(ref[:, self.at : self.at + self.rest])
        return jnp.concatenate(parts, axis=1) if len(parts) > 1 else parts[0]

    def put(self, ref, value):
        span = LANES * self.count
        ref[:, self.first * LANES : self.first * LANES + span] = value[:, :span]
        if self.rest:
            ref[:, self.at : self.at + self.rest] = value[:, span:]

    def load(self, read):
        parts = [read(t * self.rows, self.rows) for t in range(self.count)]
        if self.rest:
            packed = read(self.count * self.rows, self.group)
            rest = [packed[:, g * self.rest : (g + 1) * self.rest] for g in range(4)]
            parts.append(jnp.concatenate(rest, axis=0)[: self.rows])
        return jnp.concatenate(parts, axis=1)

    def store(self, write, value):
        for t in range(self.count):
            write(t * self.rows, self.rows, value[:, t * LANES : (t + 1) * LANES])
        if self.rest:
            rest = value[:, self.count * LANES :]
            short = 4 * self.group - self.rows
            rest = jnp.concatenate([rest, jnp.zeros((short, self.rest), rest.dtype)], axis=0)
            groups = [rest[g * self.group : (g + 1) * self.group] for g in range(4)]
            write(self.count * self.rows, self.group, jnp.concatenate(groups, axis=1))


def reader(ref, lead=(), skip=0):
    return lambda start, size: ref[(*lead, pl.ds(skip + start, size), slice(None))]


def writer(ref, lead=(), skip=0):
    def write(start, size, value):
        ref[(*lead, pl.ds(skip + start, size), slice(None))] = value

    return write


def split(value):
    high = value.astype(jnp.bfloat16)
    return high, (value - high.astype(jnp.float32)).astype(jnp.bfloat16)


def product(high, low, x_high, x_low):
    dot = functools.partial(jnp.dot, preferred_element_type=jnp.float32)
    return dot(high, x_high) + (dot(low, x_high) + dot(high, x_low))


def pack(amps, chunks):
    def kernel(amps, out):
        for chunk in chunks:
            chunk.store(writer(out, skip=chunk.start), chunk.take(amps))

    length = sum(chunk.length for chunk in chunks)
    return pl.pallas_call(
        kernel,
        in_specs=[VMEM],
        out_specs=VMEM,
        out_shape=pltpu.VMEM((length, LANES), jnp.float32),
        name="pack",
    )(pltpu.with_memory_space_constraint(amps, pltpu.VMEM))


def sum_by_source(meta, cycle_w, cycle_src, cycle_count, npair, blocks):
    nring, depth, height = cycle_w.shape
    rows = height // blocks
    tall, deep = -(-height // LANES) * LANES, -(-depth // LANES) * LANES

    def kernel(meta, src, count, w_ref, high_ref, low_ref, total, turned, ordered):
        s = pl.program_id(0)

        @pl.when(s == 0)
        def _():
            total[...] = jnp.zeros_like(total)

        @pl.when(s < count[0])
        def _():
            source = src[s]
            total[source, :depth, :height] = total[source, :depth, :height] + w_ref[0]

        @pl.when(s == nring - 1)
        def _():
            for m in range(npair):
                turned[...] = total[m].T
                for j in range(blocks):
                    start = pl.multiple_of(meta[4 + j] * rows, 8)
                    ordered[j * rows : (j + 1) * rows] = turned[pl.ds(start, rows), :depth]
                for h in range(2):
                    high_ref[m, h], low_ref[m, h] = split(ordered[h * height // 2 : (h + 1) * height // 2])

    block = pl.BlockSpec((npair, 2, height // 2, depth), lambda s, *_: (0, 0, 0, 0))
    shape = jax.ShapeDtypeStruct((npair, 2, height // 2, depth), jnp.bfloat16)
    return pl.pallas_call(
        kernel,
        grid_spec=pltpu.PrefetchScalarGridSpec(
            num_scalar_prefetch=3,
            grid=(nring,),
            in_specs=[
                pl.BlockSpec(
                    (1, depth, height), lambda s, meta, src, count: (jnp.minimum(s, count[0] - 1), 0, 0)
                )
            ],
            out_specs=[block, block],
            scratch_shapes=[
                pltpu.VMEM((npair, deep, tall), jnp.float32),
                pltpu.VMEM((tall, deep), jnp.float32),
                pltpu.VMEM((height, depth), jnp.float32),
            ],
        ),
        out_shape=[shape, shape],
        compiler_params=limit(VMEM_MIB),
        name="sum_by_source",
    )(meta, cycle_src.reshape(-1), cycle_count, cycle_w)


def ladder_weight(source, lad_src, lad_coef):
    weight = jnp.float32(0)
    for entry in range(lad_src.shape[1]):
        weight = weight + jnp.where(lad_src[0, entry] == source, lad_coef[0, entry], 0.0)
    return weight


def own_products(chunks, meta, lad_src, lad_coef, energy, weights, amps, drive, eps_row, eps_col):
    high, low = weights
    _, _, height, _ = high.shape
    rows = drive.shape[0]

    def kernel(meta, lad_src, lad_coef, energy, high, low, amps, drive, eps_row, eps_col, inverse, *outs):
        denom = eps_col[...] + eps_row[...] - energy[0]
        inverse[...] = 1.0 / denom
        weight = ladder_weight(meta[0], lad_src, lad_coef)
        for chunk, out in zip(chunks, outs, strict=True):
            mine = chunk.load(reader(amps, skip=chunk.start))
            x_high, x_low = split(mine)
            for h in range(2):
                out[h] = product(high[meta[0], h], low[meta[0], h], x_high, x_low)
            denom = eps_col[...] + chunk.take(eps_row) - energy[0]
            base = chunk.take(drive) - denom * mine + weight * mine
            out[1, height - rows :] = out[1, height - rows :] + base

    return pl.pallas_call(
        kernel,
        in_specs=[SMEM] * 4 + [VMEM] * 6,
        out_specs=[VMEM] * (1 + len(chunks)),
        out_shape=[jax.ShapeDtypeStruct(drive.shape, jnp.float32)]
        + [jax.ShapeDtypeStruct((2, height, c.width), jnp.float32) for c in chunks],
        compiler_params=limit(VMEM_MIB),
        name="own_products",
    )(meta, lad_src, lad_coef, energy, high, low, amps, drive, eps_row, eps_col)


def add_products(chunks, ks, meta, lad_src, lad_coef, weights, packed, sums):
    high, low = weights
    _, _, height, _ = high.shape
    rows = chunks[0].rows
    n = len(ks)

    def kernel(meta, lad_src, lad_coef, high, low, *refs):
        packed, refs = refs[:n], refs[n:]
        for c, chunk in enumerate(chunks):
            sums, out = refs[c :: len(chunks)]
            amps = [chunk.load(reader(ref, skip=chunk.start)) for ref in packed]
            parts = [split(x) for x in amps]
            for h in range(2):
                value = sums[h]
                for k, (x_high, x_low) in zip(ks, parts, strict=True):
                    value = value + product(high[meta[k], h], low[meta[k], h], x_high, x_low)
                out[h] = value
            value = out[1, height - rows :]
            for k, x in zip(ks, amps, strict=True):
                value = value + ladder_weight(meta[k], lad_src, lad_coef) * x
            out[1, height - rows :] = value

    return pl.pallas_call(
        kernel,
        in_specs=[SMEM] * 3 + [VMEM] * (2 + n + len(chunks)),
        out_specs=[VMEM] * len(chunks),
        out_shape=[jax.ShapeDtypeStruct(s.shape, jnp.float32) for s in sums],
        compiler_params=limit(VMEM_MIB),
        name="add_products",
    )(meta, lad_src, lad_coef, high, low, *packed, *sums)


def last_product(chunk, meta, lad_src, lad_coef, weights, amps, sums):
    high, low = weights
    npair, _, height, _ = high.shape
    rows = chunk.rows

    def kernel(meta, lad_src, lad_coef, high, low, amps, sums, *outs):
        k = meta[npair - 1]
        x = chunk.load(reader(amps))
        x_high, x_low = split(x)
        for h in range(2):
            value = sums[h] + product(high[k, h], low[k, h], x_high, x_low)
            for i in range(2):
                part = value[i * rows : (i + 1) * rows]
                if h and i:
                    part = part + ladder_weight(k, lad_src, lad_coef) * x
                chunk.store(writer(outs[2 * h + i]), part)

    outs = pl.pallas_call(
        kernel,
        in_specs=[SMEM] * 3 + [VMEM] * 4,
        out_specs=[VMEM] * 4,
        out_shape=[jax.ShapeDtypeStruct((chunk.length, LANES), jnp.float32)] * 4,
        compiler_params=limit(VMEM_MIB),
        name="last_product",
    )(meta, lad_src, lad_coef, high, low, amps, sums)
    return outs[:2], outs[2:]


def finish(chunks, done, pieces, shape, copies):
    def kernel(*refs):
        *refs, out, total_ref = refs
        total = jnp.zeros((1, LANES), jnp.float32)
        for i, chunk in enumerate(chunks):
            parts = refs[i : i + 1] if i < len(done) else refs[len(done) :]
            value = sum(chunk.load(reader(ref)) for ref in parts)
            chunk.put(out, value)
            total = total + jnp.sum(value * value)
        total_ref[...] = jnp.broadcast_to(total, total_ref.shape)

    refs = [*done, *pieces]
    return pl.pallas_call(
        kernel,
        in_specs=[VMEM] * len(refs),
        out_specs=[VMEM, VMEM],
        out_shape=[
            jax.ShapeDtypeStruct(shape, jnp.float32),
            jax.ShapeDtypeStruct((copies, 1, LANES), jnp.float32),
        ],
        compiler_params=limit(VMEM_MIB),
        name="finish",
    )(*refs)


def jacobi(residual, total, inverse, bound):
    rows, width = residual.shape
    part = rows // 5 if rows % 40 == 0 else rows

    def kernel(residual, total, inverse, residual_out, update_out, update, sems):
        copies = [pltpu.make_async_copy(residual, residual_out, sems.at[0])]
        copies[0].start()
        scale = jnp.minimum(1.0, bound / jnp.sqrt(jnp.sum(total[...], axis=0)[0:1, 0:1]))
        for start in range(0, rows, part):
            span = pl.ds(start, part)
            update[span] = (scale * residual[span]) * inverse[span]
            copies.append(pltpu.make_async_copy(update.at[span], update_out.at[span], sems.at[len(copies)]))
            copies[-1].start()
        for copy in copies:
            copy.wait()

    shape = jax.ShapeDtypeStruct(residual.shape, jnp.float32)
    return pl.pallas_call(
        kernel,
        in_specs=[VMEM, VMEM, VMEM],
        out_specs=[HBM, HBM],
        out_shape=[shape, shape],
        scratch_shapes=[
            pltpu.VMEM((rows, width), jnp.float32),
            pltpu.SemaphoreType.DMA((1 + rows // part,)),
        ],
        compiler_params=limit(VMEM_MIB),
        name="jacobi",
    )(residual, total, inverse)


def jacobi(residual, total, inverse, bound):
    def kernel(residual, total, inverse, residual_out, update_out, update, sems):
        whole = pltpu.make_async_copy(residual, residual_out, sems.at[0])
        whole.start()
        scale = jnp.minimum(1.0, bound / jnp.sqrt(jnp.sum(total[...], axis=0)[0:1, 0:1]))
        update[...] = (scale * residual[...]) * inverse[...]
        moved = pltpu.make_async_copy(update, update_out, sems.at[1])
        moved.start()
        whole.wait()
        moved.wait()

    shape = jax.ShapeDtypeStruct(residual.shape, jnp.float32)
    return pl.pallas_call(
        kernel,
        in_specs=[VMEM, VMEM, VMEM],
        out_specs=[HBM, HBM],
        out_shape=[shape, shape],
        scratch_shapes=[pltpu.VMEM(residual.shape, jnp.float32), pltpu.SemaphoreType.DMA((2,))],
        compiler_params=limit(VMEM_MIB),
        name="jacobi",
    )(residual, total, inverse)


def chain_body(amps, drive, cycle_w, cycle_src, cycle_count, ladder_src, ladder_coef, eps_vir, pair_energy):
    _, rows, width = amps.shape
    npair, blocks = lax.axis_size("occ"), width // rows
    place, chip, core = lax.axis_index("occ"), lax.axis_index("vir"), lax.axis_index("rep")
    order = [
        place,
        place ^ 1,
        place ^ 2,
        place ^ 3,
        2 * (1 - chip) + (1 - core),
        2 * chip + (1 - core),
        2 * (1 - chip) + core,
        2 * chip + core,
    ]
    meta = jnp.stack([jnp.asarray(v, jnp.int32) for v in order])
    eps_row = eps_vir.reshape(1, width)
    eps_col = lax.dynamic_slice_in_dim(eps_vir, (2 * chip + core) * rows, rows).reshape(rows, 1)

    chunks, first, start = [], 0, 0
    for count in (FIRST_TILES, width // LANES - FIRST_TILES):
        chunks.append(Chunk(rows, width, first, count, not first, start))
        first, start = first + count, start + chunks[-1].length
    own = pack(amps[0], chunks)
    far_amps = lax.ppermute(own, "occ", FAR)
    near_amps = lax.ppermute(own, "occ", NEAR)
    weights = sum_by_source(meta, jnp.swapaxes(cycle_w[0], 1, 2), cycle_src, cycle_count, npair, blocks)
    inverse, *sums = own_products(
        chunks, meta, ladder_src, ladder_coef, pair_energy, weights, own, drive[0], eps_row, eps_col
    )
    far_amps, sums = lax.optimization_barrier((far_amps, sums))
    sums = add_products(
        chunks, (1, 2), meta, ladder_src, ladder_coef, weights, (near_amps, far_amps), sums
    )
    outgoing = [far_amps[c.start : c.start + c.length] for c in chunks]
    outgoing[1:], sums = lax.optimization_barrier((outgoing[1:], sums))
    last_amps = [lax.ppermute(x, "occ", NEAR) for x in outgoing]

    done = []
    for i, chunk in enumerate(chunks):
        away, keep = last_product(chunk, meta, ladder_src, ladder_coef, weights, last_amps[i], sums[i])
        got = [lax.ppermute(x, "rep", SWAP) for x in away]
        for_far = keep[0] + got[0]
        done, for_far = lax.optimization_barrier((done, for_far))
        far = lax.ppermute(for_far, "vir", SWAP)
        pieces = (keep[1], got[1], far)
        if i < len(chunks) - 1:
            done.append(sum(pieces))
    residual, total = finish(chunks, done, pieces, (rows, width), npair * blocks)
    total = lax.all_to_all(total, ("occ", "vir", "rep"), split_axis=0, concat_axis=0, tiled=True)
    residual, update = jacobi(residual, total, inverse, clip_level * width * math.sqrt(npair))
    return residual[None], update[None]


def any_body(amps, drive, cycle_w, cycle_src, cycle_count, ladder_src, ladder_coef, eps_vir, pair_energy):
    largest_value = lax.Precision.HIGHEST
    pairs_per_unit, rows, width = amps.shape
    nring = cycle_w.shape[1]
    npair = pairs_per_unit * lax.axis_size("occ")
    all_rows = lax.all_gather(amps, "occ", axis=0, tiled=True)
    ladder = jnp.sum(ladder_coef[:, :, None, None] * all_rows[ladder_src], axis=1)
    selected_rows = jnp.take(all_rows, cycle_src.reshape(-1), axis=0).reshape(
        pairs_per_unit, nring, rows, width
    )
    live = (jnp.arange(nring)[None, :] < cycle_count[:, None]).astype(jnp.float32)
    partial_value = jnp.einsum(
        "ptac,ptcb->pab", cycle_w * live[:, :, None, None], selected_rows, precision=largest_value
    )
    cycle = lax.psum_scatter(partial_value, ("vir", "rep"), scatter_dimension=1, tiled=True)
    first_row = lax.axis_index(("vir", "rep")) * rows
    eps_rows = lax.dynamic_slice_in_dim(eps_vir, first_row, rows)
    denom = eps_rows[None, :, None] + eps_vir[None, None, :] - pair_energy[:, None, None]
    residual = drive + cycle + ladder - denom * amps
    total = lax.psum(jnp.sum(residual * residual), ("occ", "vir", "rep"))
    scale = jnp.minimum(1.0, clip_level * width * math.sqrt(npair) / jnp.sqrt(total))
    return residual, scale * residual / denom


def body(*args):
    amps, cycle_w = args[0], args[2]
    pairs_per_unit, rows, width = amps.shape
    chain = (
        pairs_per_unit == 1
        and (lax.axis_size("occ"), lax.axis_size("vir"), lax.axis_size("rep")) == (4, 2, 2)
        and cycle_w.shape[1] >= 4
        and rows % 8 == 0
        and width % LANES == LANES // 4
        and width > (FIRST_TILES + 1) * LANES
    )
    return (chain_body if chain else any_body)(*args)


def solution(mesh):
    in_specs = (
        P(("groups", "occ"), ("vir", "rep"), None),
        P(("groups", "occ"), ("vir", "rep"), None),
        P(("groups", "occ"), None, None, ("vir", "rep")),
        P(("groups", "occ"), None),
        P(("groups", "occ")),
        P(("groups", "occ"), None),
        P(("groups", "occ"), None),
        P("groups"),
        P(("groups", "occ")),
    )
    out_specs = (
        P(("groups", "occ"), ("vir", "rep"), None),
        P(("groups", "occ"), ("vir", "rep"), None),
    )
    return jax.shard_map(body, mesh=mesh, in_specs=in_specs, out_specs=out_specs, check_vma=False)
```

```python
import functools
import math

import jax
import jax.numpy as jnp
from jax import lax
from jax.experimental import pallas as pl
from jax.experimental.pallas import tpu as pltpu
from jax.sharding import PartitionSpec as P

clip_level = 0.5
LANES = 128
SMEM = pl.BlockSpec(memory_space=pltpu.SMEM)
VMEM = pl.BlockSpec(memory_space=pltpu.VMEM)
HBM = pl.BlockSpec(memory_space=pl.ANY)
SWAP = [(0, 1), (1, 0)]
NEAR = [(0, 1), (1, 0), (2, 3), (3, 2)]
FAR = [(0, 2), (2, 0), (1, 3), (3, 1)]
VMEM_MIB = 20
FIRST_TILES = 2


def limit(n):
    return pltpu.CompilerParams(vmem_limit_bytes=n << 20)


class Chunk:
    def __init__(self, rows, width, first, count, rest, start):
        self.rows, self.first, self.count, self.start = rows, first, count, start
        self.rest = width % LANES if rest else 0
        self.at = width - self.rest
        self.group = -(-rows // 32) * 8
        self.length = rows * count + (self.group if self.rest else 0)
        self.width = LANES * count + self.rest

    def take(self, ref):
        parts = [ref[:, self.first * LANES : (self.first + self.count) * LANES]]
        if self.rest:
            parts.append(ref[:, self.at : self.at + self.rest])
        return jnp.concatenate(parts, axis=1) if len(parts) > 1 else parts[0]

    def put(self, ref, value):
        span = LANES * self.count
        ref[:, self.first * LANES : self.first * LANES + span] = value[:, :span]
        if self.rest:
            ref[:, self.at : self.at + self.rest] = value[:, span:]

    def load(self, read):
        parts = [read(t * self.rows, self.rows) for t in range(self.count)]
        if self.rest:
            packed = read(self.count * self.rows, self.group)
            rest = [packed[:, g * self.rest : (g + 1) * self.rest] for g in range(4)]
            parts.append(jnp.concatenate(rest, axis=0)[: self.rows])
        return jnp.concatenate(parts, axis=1)

    def store(self, write, value):
        for t in range(self.count):
            write(t * self.rows, self.rows, value[:, t * LANES : (t + 1) * LANES])
        if self.rest:
            rest = value[:, self.count * LANES :]
            short = 4 * self.group - self.rows
            rest = jnp.concatenate([rest, jnp.zeros((short, self.rest), rest.dtype)], axis=0)
            groups = [rest[g * self.group : (g + 1) * self.group] for g in range(4)]
            write(self.count * self.rows, self.group, jnp.concatenate(groups, axis=1))


def reader(ref, lead=(), skip=0):
    return lambda start, size: ref[(*lead, pl.ds(skip + start, size), slice(None))]


def writer(ref, lead=(), skip=0):
    def write(start, size, value):
        ref[(*lead, pl.ds(skip + start, size), slice(None))] = value

    return write


def split(value):
    high = value.astype(jnp.bfloat16)
    return high, (value - high.astype(jnp.float32)).astype(jnp.bfloat16)


def product(weights, x_high, x_low):
    rows = weights.shape[0] // 2
    dot = functools.partial(jnp.dot, preferred_element_type=jnp.float32)
    value = dot(weights, x_high)
    return value[:rows] + (value[rows:] + dot(weights[:rows], x_low))


def pack(amps, chunks):
    def kernel(amps, out):
        for chunk in chunks:
            chunk.store(writer(out, skip=chunk.start), chunk.take(amps))

    length = sum(chunk.length for chunk in chunks)
    return pl.pallas_call(
        kernel,
        in_specs=[VMEM],
        out_specs=VMEM,
        out_shape=pltpu.VMEM((length, LANES), jnp.float32),
        name="pack",
    )(pltpu.with_memory_space_constraint(amps, pltpu.VMEM))


def sum_by_source(meta, cycle_w, cycle_src, cycle_count, npair, blocks):
    nring, depth, height = cycle_w.shape
    rows = height // blocks
    tall, deep = -(-height // LANES) * LANES, -(-depth // LANES) * LANES

    def kernel(meta, src, count, w_ref, out, total, turned, ordered):
        s = pl.program_id(0)

        @pl.when(s == 0)
        def _():
            total[...] = jnp.zeros_like(total)

        @pl.when(s < count[0])
        def _():
            source = src[s]
            total[source, :depth, :height] = total[source, :depth, :height] + w_ref[0]

        @pl.when(s == nring - 1)
        def _():
            for m in range(npair):
                turned[...] = total[m].T
                for j in range(blocks):
                    start = pl.multiple_of(meta[4 + j] * rows, 8)
                    ordered[j * rows : (j + 1) * rows] = turned[pl.ds(start, rows), :depth]
                for h in range(2):
                    high, low = split(ordered[h * height // 2 : (h + 1) * height // 2])
                    out[m, h, : height // 2] = high
                    out[m, h, height // 2 :] = low

    shape = (npair, 2, height, depth)
    return pl.pallas_call(
        kernel,
        grid_spec=pltpu.PrefetchScalarGridSpec(
            num_scalar_prefetch=3,
            grid=(nring,),
            in_specs=[
                pl.BlockSpec(
                    (1, depth, height), lambda s, meta, src, count: (jnp.minimum(s, count[0] - 1), 0, 0)
                )
            ],
            out_specs=pl.BlockSpec(shape, lambda s, *_: (0, 0, 0, 0)),
            scratch_shapes=[
                pltpu.VMEM((npair, deep, tall), jnp.float32),
                pltpu.VMEM((tall, deep), jnp.float32),
                pltpu.VMEM((height, depth), jnp.float32),
            ],
        ),
        out_shape=jax.ShapeDtypeStruct(shape, jnp.bfloat16),
        compiler_params=limit(VMEM_MIB),
        name="sum_by_source",
    )(meta, cycle_src.reshape(-1), cycle_count, cycle_w)


def ladder_weight(source, lad_src, lad_coef):
    weight = jnp.float32(0)
    for entry in range(lad_src.shape[1]):
        weight = weight + jnp.where(lad_src[0, entry] == source, lad_coef[0, entry], 0.0)
    return weight


def own_products(chunks, meta, lad_src, lad_coef, energy, weights, amps, drive, eps_row, eps_col):
    height = weights.shape[2] // 2
    rows = drive.shape[0]

    def kernel(meta, lad_src, lad_coef, energy, weights, amps, drive, eps_row, eps_col, inverse, *outs):
        denom = eps_col[...] + eps_row[...] - energy[0]
        inverse[...] = 1.0 / denom
        weight = ladder_weight(meta[0], lad_src, lad_coef)
        for chunk, out in zip(chunks, outs, strict=True):
            mine = chunk.load(reader(amps, skip=chunk.start))
            x_high, x_low = split(mine)
            for h in range(2):
                out[h] = product(weights[meta[0], h], x_high, x_low)
            denom = eps_col[...] + chunk.take(eps_row) - energy[0]
            base = chunk.take(drive) - denom * mine + weight * mine
            out[1, height - rows :] = out[1, height - rows :] + base

    return pl.pallas_call(
        kernel,
        in_specs=[SMEM] * 4 + [VMEM] * 5,
        out_specs=[VMEM] * (1 + len(chunks)),
        out_shape=[jax.ShapeDtypeStruct(drive.shape, jnp.float32)]
        + [jax.ShapeDtypeStruct((2, height, c.width), jnp.float32) for c in chunks],
        compiler_params=limit(VMEM_MIB),
        name="own_products",
    )(meta, lad_src, lad_coef, energy, weights, amps, drive, eps_row, eps_col)


def add_products(chunks, ks, meta, lad_src, lad_coef, weights, packed, sums):
    height = weights.shape[2] // 2
    rows = chunks[0].rows
    n = len(ks)

    def kernel(meta, lad_src, lad_coef, weights, *refs):
        packed, refs = refs[:n], refs[n:]
        for c, chunk in enumerate(chunks):
            sums, out = refs[c :: len(chunks)]
            amps = [chunk.load(reader(ref, skip=chunk.start)) for ref in packed]
            parts = [split(x) for x in amps]
            for h in range(2):
                value = sums[h]
                for k, (x_high, x_low) in zip(ks, parts, strict=True):
                    value = value + product(weights[meta[k], h], x_high, x_low)
                out[h] = value
            value = out[1, height - rows :]
            for k, x in zip(ks, amps, strict=True):
                value = value + ladder_weight(meta[k], lad_src, lad_coef) * x
            out[1, height - rows :] = value

    return pl.pallas_call(
        kernel,
        in_specs=[SMEM] * 3 + [VMEM] * (1 + n + len(chunks)),
        out_specs=[VMEM] * len(chunks),
        out_shape=[jax.ShapeDtypeStruct(s.shape, jnp.float32) for s in sums],
        compiler_params=limit(VMEM_MIB),
        name="add_products",
    )(meta, lad_src, lad_coef, weights, *packed, *sums)


def last_product(chunk, half, meta, lad_src, lad_coef, weights, amps, sums):
    npair, height = weights.shape[0], weights.shape[2] // 2
    rows = chunk.rows

    def kernel(meta, lad_src, lad_coef, weights, amps, sums, *outs):
        k = meta[npair - 1]
        x = chunk.load(reader(amps))
        x_high, x_low = split(x)
        value = sums[half] + product(weights[k, half], x_high, x_low)
        for i in range(2):
            part = value[i * rows : (i + 1) * rows]
            if half and i:
                part = part + ladder_weight(k, lad_src, lad_coef) * x
            chunk.store(writer(outs[i]), part)

    return pl.pallas_call(
        kernel,
        in_specs=[SMEM] * 3 + [VMEM] * 3,
        out_specs=[VMEM] * 2,
        out_shape=[jax.ShapeDtypeStruct((chunk.length, LANES), jnp.float32)] * 2,
        compiler_params=limit(VMEM_MIB),
        name="last_product",
    )(meta, lad_src, lad_coef, weights, amps, sums)


def finish(chunks, done, pieces, shape, copies):
    def kernel(*refs):
        *refs, out, total_ref = refs
        total = jnp.zeros((1, LANES), jnp.float32)
        for i, chunk in enumerate(chunks):
            parts = refs[i : i + 1] if i < len(done) else refs[len(done) :]
            value = sum(chunk.load(reader(ref)) for ref in parts)
            chunk.put(out, value)
            total = total + jnp.sum(value * value)
        total_ref[...] = jnp.broadcast_to(total, total_ref.shape)

    refs = [*done, *pieces]
    return pl.pallas_call(
        kernel,
        in_specs=[VMEM] * len(refs),
        out_specs=[VMEM, VMEM],
        out_shape=[
            jax.ShapeDtypeStruct(shape, jnp.float32),
            jax.ShapeDtypeStruct((copies, 1, LANES), jnp.float32),
        ],
        compiler_params=limit(VMEM_MIB),
        name="finish",
    )(*refs)


def jacobi(residual, total, inverse, bound):
    rows, width = residual.shape
    part = rows // 5 if rows % 40 == 0 else rows

    def kernel(residual, total, inverse, residual_out, update_out, update, sems):
        copies = [pltpu.make_async_copy(residual, residual_out, sems.at[0])]
        copies[0].start()
        scale = jnp.minimum(1.0, bound / jnp.sqrt(jnp.sum(total[...], axis=0)[0:1, 0:1]))
        for start in range(0, rows, part):
            span = pl.ds(start, part)
            update[span] = (scale * residual[span]) * inverse[span]
            copies.append(pltpu.make_async_copy(update.at[span], update_out.at[span], sems.at[len(copies)]))
            copies[-1].start()
        for copy in copies:
            copy.wait()

    shape = jax.ShapeDtypeStruct(residual.shape, jnp.float32)
    return pl.pallas_call(
        kernel,
        in_specs=[VMEM, VMEM, VMEM],
        out_specs=[HBM, HBM],
        out_shape=[shape, shape],
        scratch_shapes=[
            pltpu.VMEM((rows, width), jnp.float32),
            pltpu.SemaphoreType.DMA((1 + rows // part,)),
        ],
        compiler_params=limit(VMEM_MIB),
        name="jacobi",
    )(residual, total, inverse)


def jacobi(residual, total, inverse, bound):
    def kernel(residual, total, inverse, residual_out, update_out, update, sems):
        whole = pltpu.make_async_copy(residual, residual_out, sems.at[0])
        whole.start()
        scale = jnp.minimum(1.0, bound / jnp.sqrt(jnp.sum(total[...], axis=0)[0:1, 0:1]))
        update[...] = (scale * residual[...]) * inverse[...]
        moved = pltpu.make_async_copy(update, update_out, sems.at[1])
        moved.start()
        whole.wait()
        moved.wait()

    shape = jax.ShapeDtypeStruct(residual.shape, jnp.float32)
    return pl.pallas_call(
        kernel,
        in_specs=[VMEM, VMEM, VMEM],
        out_specs=[HBM, HBM],
        out_shape=[shape, shape],
        scratch_shapes=[pltpu.VMEM(residual.shape, jnp.float32), pltpu.SemaphoreType.DMA((2,))],
        compiler_params=limit(VMEM_MIB),
        name="jacobi",
    )(residual, total, inverse)


def chain_body(amps, drive, cycle_w, cycle_src, cycle_count, ladder_src, ladder_coef, eps_vir, pair_energy):
    _, rows, width = amps.shape
    npair, blocks = lax.axis_size("occ"), width // rows
    place, chip, core = lax.axis_index("occ"), lax.axis_index("vir"), lax.axis_index("rep")
    order = [
        place,
        place ^ 1,
        place ^ 2,
        place ^ 3,
        2 * (1 - chip) + (1 - core),
        2 * chip + (1 - core),
        2 * (1 - chip) + core,
        2 * chip + core,
    ]
    meta = jnp.stack([jnp.asarray(v, jnp.int32) for v in order])
    eps_row = eps_vir.reshape(1, width)
    eps_col = lax.dynamic_slice_in_dim(eps_vir, (2 * chip + core) * rows, rows).reshape(rows, 1)

    chunks, first, start = [], 0, 0
    for count in (FIRST_TILES, width // LANES - FIRST_TILES):
        chunks.append(Chunk(rows, width, first, count, not first, start))
        first, start = first + count, start + chunks[-1].length
    own = pack(amps[0], chunks)
    far_amps = lax.ppermute(own, "occ", FAR)
    near_amps = lax.ppermute(own, "occ", NEAR)
    weights = sum_by_source(meta, jnp.swapaxes(cycle_w[0], 1, 2), cycle_src, cycle_count, npair, blocks)
    inverse, *sums = own_products(
        chunks, meta, ladder_src, ladder_coef, pair_energy, weights, own, drive[0], eps_row, eps_col
    )
    far_amps, sums = lax.optimization_barrier((far_amps, sums))
    sums = add_products(
        chunks, (1, 2), meta, ladder_src, ladder_coef, weights, (near_amps, far_amps), sums
    )
    outgoing = [far_amps[c.start : c.start + c.length] for c in chunks]
    outgoing[1:], sums = lax.optimization_barrier((outgoing[1:], sums))
    last_amps = [lax.ppermute(x, "occ", NEAR) for x in outgoing]

    done = []
    for i, chunk in enumerate(chunks):
        away, keep = [
            last_product(chunk, half, meta, ladder_src, ladder_coef, weights, last_amps[i], sums[i])
            for half in range(2)
        ]
        got = [lax.ppermute(x, "rep", SWAP) for x in away]
        for_far = keep[0] + got[0]
        done, for_far = lax.optimization_barrier((done, for_far))
        far = lax.ppermute(for_far, "vir", SWAP)
        pieces = (keep[1], got[1], far)
        if i < len(chunks) - 1:
            done.append(sum(pieces))
    residual, total = finish(chunks, done, pieces, (rows, width), npair * blocks)
    total = lax.all_to_all(total, ("occ", "vir", "rep"), split_axis=0, concat_axis=0, tiled=True)
    residual, update = jacobi(residual, total, inverse, clip_level * width * math.sqrt(npair))
    return residual[None], update[None]


def any_body(amps, drive, cycle_w, cycle_src, cycle_count, ladder_src, ladder_coef, eps_vir, pair_energy):
    largest_value = lax.Precision.HIGHEST
    pairs_per_unit, rows, width = amps.shape
    nring = cycle_w.shape[1]
    npair = pairs_per_unit * lax.axis_size("occ")
    all_rows = lax.all_gather(amps, "occ", axis=0, tiled=True)
    ladder = jnp.sum(ladder_coef[:, :, None, None] * all_rows[ladder_src], axis=1)
    selected_rows = jnp.take(all_rows, cycle_src.reshape(-1), axis=0).reshape(
        pairs_per_unit, nring, rows, width
    )
    live = (jnp.arange(nring)[None, :] < cycle_count[:, None]).astype(jnp.float32)
    partial_value = jnp.einsum(
        "ptac,ptcb->pab", cycle_w * live[:, :, None, None], selected_rows, precision=largest_value
    )
    cycle = lax.psum_scatter(partial_value, ("vir", "rep"), scatter_dimension=1, tiled=True)
    first_row = lax.axis_index(("vir", "rep")) * rows
    eps_rows = lax.dynamic_slice_in_dim(eps_vir, first_row, rows)
    denom = eps_rows[None, :, None] + eps_vir[None, None, :] - pair_energy[:, None, None]
    residual = drive + cycle + ladder - denom * amps
    total = lax.psum(jnp.sum(residual * residual), ("occ", "vir", "rep"))
    scale = jnp.minimum(1.0, clip_level * width * math.sqrt(npair) / jnp.sqrt(total))
    return residual, scale * residual / denom


def body(*args):
    amps, cycle_w = args[0], args[2]
    pairs_per_unit, rows, width = amps.shape
    chain = (
        pairs_per_unit == 1
        and (lax.axis_size("occ"), lax.axis_size("vir"), lax.axis_size("rep")) == (4, 2, 2)
        and cycle_w.shape[1] >= 4
        and rows % 8 == 0
        and width % LANES == LANES // 4
        and width > (FIRST_TILES + 1) * LANES
    )
    return (chain_body if chain else any_body)(*args)


def solution(mesh):
    in_specs = (
        P(("groups", "occ"), ("vir", "rep"), None),
        P(("groups", "occ"), ("vir", "rep"), None),
        P(("groups", "occ"), None, None, ("vir", "rep")),
        P(("groups", "occ"), None),
        P(("groups", "occ")),
        P(("groups", "occ"), None),
        P(("groups", "occ"), None),
        P("groups"),
        P(("groups", "occ")),
    )
    out_specs = (
        P(("groups", "occ"), ("vir", "rep"), None),
        P(("groups", "occ"), ("vir", "rep"), None),
    )
    return jax.shard_map(body, mesh=mesh, in_specs=in_specs, out_specs=out_specs, check_vma=False)
```

```python
import functools
import math

import jax
import jax.numpy as jnp
from jax import lax
from jax.experimental import pallas as pl
from jax.experimental.pallas import tpu as pltpu
from jax.sharding import PartitionSpec as P

clip_level = 0.5
LANES = 128
SMEM = pl.BlockSpec(memory_space=pltpu.SMEM)
VMEM = pl.BlockSpec(memory_space=pltpu.VMEM)
HBM = pl.BlockSpec(memory_space=pl.ANY)
SWAP = [(0, 1), (1, 0)]
NEAR = [(0, 1), (1, 0), (2, 3), (3, 2)]
FAR = [(0, 2), (2, 0), (1, 3), (3, 1)]
VMEM_MIB = 20


def limit(n):
    return pltpu.CompilerParams(vmem_limit_bytes=n << 20)


class Chunk:
    def __init__(self, rows, width, first, count, rest, start):
        self.rows, self.first, self.count, self.start = rows, first, count, start
        self.rest = width % LANES if rest else 0
        self.at = width - self.rest
        self.group = -(-rows // 32) * 8
        self.length = rows * count + (self.group if self.rest else 0)
        self.width = LANES * count + self.rest

    def take(self, ref):
        parts = [ref[:, self.first * LANES : (self.first + self.count) * LANES]]
        if self.rest:
            parts.append(ref[:, self.at : self.at + self.rest])
        return jnp.concatenate(parts, axis=1) if len(parts) > 1 else parts[0]

    def put(self, ref, value):
        span = LANES * self.count
        ref[:, self.first * LANES : self.first * LANES + span] = value[:, :span]
        if self.rest:
            ref[:, self.at : self.at + self.rest] = value[:, span:]

    def load(self, read):
        parts = [read(t * self.rows, self.rows) for t in range(self.count)]
        if self.rest:
            packed = read(self.count * self.rows, self.group)
            rest = [packed[:, g * self.rest : (g + 1) * self.rest] for g in range(4)]
            parts.append(jnp.concatenate(rest, axis=0)[: self.rows])
        return jnp.concatenate(parts, axis=1)

    def store(self, write, value):
        for t in range(self.count):
            write(t * self.rows, self.rows, value[:, t * LANES : (t + 1) * LANES])
        if self.rest:
            rest = value[:, self.count * LANES :]
            short = 4 * self.group - self.rows
            rest = jnp.concatenate([rest, jnp.zeros((short, self.rest), rest.dtype)], axis=0)
            groups = [rest[g * self.group : (g + 1) * self.group] for g in range(4)]
            write(self.count * self.rows, self.group, jnp.concatenate(groups, axis=1))


def reader(ref, lead=(), skip=0):
    return lambda start, size: ref[(*lead, pl.ds(skip + start, size), slice(None))]


def writer(ref, lead=(), skip=0):
    def write(start, size, value):
        ref[(*lead, pl.ds(skip + start, size), slice(None))] = value

    return write


def split(value):
    high = value.astype(jnp.bfloat16)
    return high, (value - high.astype(jnp.float32)).astype(jnp.bfloat16)


def product(weights, x_high, x_low):
    rows = weights.shape[0] // 2
    dot = functools.partial(jnp.dot, preferred_element_type=jnp.float32)
    value = dot(weights, x_high)
    return value[:rows] + (value[rows:] + dot(weights[:rows], x_low))


def pack(amps, chunks):
    def kernel(amps, out):
        for chunk in chunks:
            chunk.store(writer(out, skip=chunk.start), chunk.take(amps))

    length = sum(chunk.length for chunk in chunks)
    return pl.pallas_call(
        kernel,
        in_specs=[VMEM],
        out_specs=VMEM,
        out_shape=pltpu.VMEM((length, LANES), jnp.float32),
        compiler_params=limit(VMEM_MIB),
        name="pack",
    )(pltpu.with_memory_space_constraint(amps, pltpu.VMEM))


def sum_by_source(meta, cycle_w, cycle_src, cycle_count, npair, blocks):
    nring, depth, height = cycle_w.shape
    rows = height // blocks
    tall, deep = -(-height // LANES) * LANES, -(-depth // LANES) * LANES

    def kernel(meta, src, count, w_ref, out, total, turned, ordered):
        s = pl.program_id(0)

        @pl.when(s == 0)
        def _():
            total[...] = jnp.zeros_like(total)

        @pl.when(s < count[0])
        def _():
            source = src[s]
            total[source, :depth, :height] = total[source, :depth, :height] + w_ref[0]

        @pl.when(s == nring - 1)
        def _():
            for m in range(npair):
                turned[...] = total[m].T
                for j in range(blocks):
                    start = pl.multiple_of(meta[4 + j] * rows, 8)
                    ordered[j * rows : (j + 1) * rows] = turned[pl.ds(start, rows), :depth]
                for h in range(2):
                    high, low = split(ordered[h * height // 2 : (h + 1) * height // 2])
                    out[m, h, : height // 2] = high
                    out[m, h, height // 2 :] = low

    shape = (npair, 2, height, depth)
    return pl.pallas_call(
        kernel,
        grid_spec=pltpu.PrefetchScalarGridSpec(
            num_scalar_prefetch=3,
            grid=(nring,),
            in_specs=[
                pl.BlockSpec(
                    (1, depth, height), lambda s, meta, src, count: (jnp.minimum(s, count[0] - 1), 0, 0)
                )
            ],
            out_specs=pl.BlockSpec(shape, lambda s, *_: (0, 0, 0, 0)),
            scratch_shapes=[
                pltpu.VMEM((npair, deep, tall), jnp.float32),
                pltpu.VMEM((tall, deep), jnp.float32),
                pltpu.VMEM((height, depth), jnp.float32),
            ],
        ),
        out_shape=jax.ShapeDtypeStruct(shape, jnp.bfloat16),
        compiler_params=limit(VMEM_MIB),
        name="sum_by_source",
    )(meta, cycle_src.reshape(-1), cycle_count, cycle_w)


def ladder_weight(source, lad_src, lad_coef):
    weight = jnp.float32(0)
    for entry in range(lad_src.shape[1]):
        weight = weight + jnp.where(lad_src[0, entry] == source, lad_coef[0, entry], 0.0)
    return weight


def own_products(chunks, meta, lad_src, lad_coef, energy, weights, amps, drive, eps_row, eps_col):
    height = weights.shape[2] // 2
    rows = drive.shape[0]

    def kernel(meta, lad_src, lad_coef, energy, weights, amps, drive, eps_row, eps_col, inverse, *outs):
        denom = eps_col[...] + eps_row[...] - energy[0]
        inverse[...] = 1.0 / denom
        weight = ladder_weight(meta[0], lad_src, lad_coef)
        for chunk, out in zip(chunks, outs, strict=True):
            mine = chunk.load(reader(amps, skip=chunk.start))
            x_high, x_low = split(mine)
            for h in range(2):
                out[h] = product(weights[meta[0], h], x_high, x_low)
            denom = eps_col[...] + chunk.take(eps_row) - energy[0]
            base = chunk.take(drive) - denom * mine + weight * mine
            out[1, height - rows :] = out[1, height - rows :] + base

    return pl.pallas_call(
        kernel,
        in_specs=[SMEM] * 4 + [VMEM] * 5,
        out_specs=[VMEM] * (1 + len(chunks)),
        out_shape=[jax.ShapeDtypeStruct(drive.shape, jnp.float32)]
        + [jax.ShapeDtypeStruct((2, height, c.width), jnp.float32) for c in chunks],
        compiler_params=limit(VMEM_MIB),
        name="own_products",
    )(meta, lad_src, lad_coef, energy, weights, amps, drive, eps_row, eps_col)


def add_products(chunks, ks, meta, lad_src, lad_coef, weights, packed, sums):
    height = weights.shape[2] // 2
    rows = chunks[0].rows
    n = len(ks)

    def kernel(meta, lad_src, lad_coef, weights, *refs):
        packed, refs = refs[:n], refs[n:]
        for c, chunk in enumerate(chunks):
            sums, out = refs[c :: len(chunks)]
            amps = [chunk.load(reader(ref, skip=chunk.start)) for ref in packed]
            parts = [split(x) for x in amps]
            for h in range(2):
                value = sums[h]
                for k, (x_high, x_low) in zip(ks, parts, strict=True):
                    value = value + product(weights[meta[k], h], x_high, x_low)
                out[h] = value
            value = out[1, height - rows :]
            for k, x in zip(ks, amps, strict=True):
                value = value + ladder_weight(meta[k], lad_src, lad_coef) * x
            out[1, height - rows :] = value

    return pl.pallas_call(
        kernel,
        in_specs=[SMEM] * 3 + [VMEM] * (1 + n + len(chunks)),
        out_specs=[VMEM] * len(chunks),
        out_shape=[jax.ShapeDtypeStruct(s.shape, jnp.float32) for s in sums],
        compiler_params=limit(VMEM_MIB),
        name="add_products",
    )(meta, lad_src, lad_coef, weights, *packed, *sums)


def last_product(chunk, halves, meta, lad_src, lad_coef, weights, amps, sums):
    npair, height = weights.shape[0], weights.shape[2] // 2
    rows = chunk.rows

    def kernel(meta, lad_src, lad_coef, weights, amps, sums, *outs):
        k = meta[npair - 1]
        x = chunk.load(reader(amps))
        x_high, x_low = split(x)
        for n, half in enumerate(halves):
            value = sums[half] + product(weights[k, half], x_high, x_low)
            for i in range(2):
                part = value[i * rows : (i + 1) * rows]
                if half and i:
                    part = part + ladder_weight(k, lad_src, lad_coef) * x
                chunk.store(writer(outs[2 * n + i]), part)

    outs = pl.pallas_call(
        kernel,
        in_specs=[SMEM] * 3 + [VMEM] * 3,
        out_specs=[VMEM] * (2 * len(halves)),
        out_shape=[jax.ShapeDtypeStruct((chunk.length, LANES), jnp.float32)] * (2 * len(halves)),
        compiler_params=limit(VMEM_MIB),
        name="last_product",
    )(meta, lad_src, lad_coef, weights, amps, sums)
    return [list(outs[2 * n : 2 * n + 2]) for n in range(len(halves))]


def from_other_core(parts):
    n = parts[0].shape[0]
    both = lax.all_gather(jnp.concatenate(parts), "rep", axis=0, tiled=True)
    total = 0.5 * both[: 2 * n] + 0.5 * both[2 * n :]
    return [2.0 * (total[i * n : (i + 1) * n] - 0.5 * part) for i, part in enumerate(parts)]


def finish(chunks, done, pieces, shape, copies):
    def kernel(*refs):
        *refs, out, total_ref = refs
        total = jnp.zeros((1, LANES), jnp.float32)
        for i, chunk in enumerate(chunks):
            parts = refs[i : i + 1] if i < len(done) else refs[len(done) :]
            value = sum(chunk.load(reader(ref)) for ref in parts)
            chunk.put(out, value)
            total = total + jnp.sum(value * value)
        total_ref[...] = jnp.broadcast_to(total, total_ref.shape)

    refs = [*done, *pieces]
    return pl.pallas_call(
        kernel,
        in_specs=[VMEM] * len(refs),
        out_specs=[VMEM, VMEM],
        out_shape=[
            jax.ShapeDtypeStruct(shape, jnp.float32),
            jax.ShapeDtypeStruct((copies, 1, LANES), jnp.float32),
        ],
        compiler_params=limit(VMEM_MIB),
        name="finish",
    )(*refs)


def jacobi(residual, total, inverse, bound):
    rows, width = residual.shape
    part = rows // 5 if rows % 40 == 0 else rows

    def kernel(residual, total, inverse, residual_out, update_out, update, sems):
        copies = [pltpu.make_async_copy(residual, residual_out, sems.at[0])]
        copies[0].start()
        scale = jnp.minimum(1.0, bound / jnp.sqrt(jnp.sum(total[...], axis=0)[0:1, 0:1]))
        for start in range(0, rows, part):
            span = pl.ds(start, part)
            update[span] = (scale * residual[span]) * inverse[span]
            copies.append(pltpu.make_async_copy(update.at[span], update_out.at[span], sems.at[len(copies)]))
            copies[-1].start()
        for copy in copies:
            copy.wait()

    shape = jax.ShapeDtypeStruct(residual.shape, jnp.float32)
    return pl.pallas_call(
        kernel,
        in_specs=[VMEM, VMEM, VMEM],
        out_specs=[HBM, HBM],
        out_shape=[shape, shape],
        scratch_shapes=[
            pltpu.VMEM((rows, width), jnp.float32),
            pltpu.SemaphoreType.DMA((1 + rows // part,)),
        ],
        compiler_params=limit(VMEM_MIB),
        name="jacobi",
    )(residual, total, inverse)


def jacobi(residual, total, inverse, bound):
    def kernel(residual, total, inverse, residual_out, update_out, update, sems):
        whole = pltpu.make_async_copy(residual, residual_out, sems.at[0])
        whole.start()
        scale = jnp.minimum(1.0, bound / jnp.sqrt(jnp.sum(total[...], axis=0)[0:1, 0:1]))
        update[...] = (scale * residual[...]) * inverse[...]
        moved = pltpu.make_async_copy(update, update_out, sems.at[1])
        moved.start()
        whole.wait()
        moved.wait()

    shape = jax.ShapeDtypeStruct(residual.shape, jnp.float32)
    return pl.pallas_call(
        kernel,
        in_specs=[VMEM, VMEM, VMEM],
        out_specs=[HBM, HBM],
        out_shape=[shape, shape],
        scratch_shapes=[pltpu.VMEM(residual.shape, jnp.float32), pltpu.SemaphoreType.DMA((2,))],
        compiler_params=limit(VMEM_MIB),
        name="jacobi",
    )(residual, total, inverse)


def chain_body(amps, drive, cycle_w, cycle_src, cycle_count, ladder_src, ladder_coef, eps_vir, pair_energy):
    _, rows, width = amps.shape
    npair, blocks = lax.axis_size("occ"), width // rows
    place, chip, core = lax.axis_index("occ"), lax.axis_index("vir"), lax.axis_index("rep")
    order = [
        place,
        place ^ 1,
        place ^ 2,
        place ^ 3,
        2 * (1 - chip) + (1 - core),
        2 * chip + (1 - core),
        2 * (1 - chip) + core,
        2 * chip + core,
    ]
    meta = jnp.stack([jnp.asarray(v, jnp.int32) for v in order])
    eps_row = eps_vir.reshape(1, width)
    eps_col = lax.dynamic_slice_in_dim(eps_vir, (2 * chip + core) * rows, rows).reshape(rows, 1)

    chunks, first, start = [], 0, 0
    third = width // LANES // 3
    for count in (third, third, width // LANES - 2 * third):
        chunks.append(Chunk(rows, width, first, count, first + count == width // LANES, start))
        first, start = first + count, start + chunks[-1].length
    own = pack(amps[0], chunks)
    far_amps = lax.ppermute(own, "occ", FAR)
    near_amps = lax.ppermute(own, "occ", NEAR)
    weights = sum_by_source(meta, jnp.swapaxes(cycle_w[0], 1, 2), cycle_src, cycle_count, npair, blocks)
    inverse, *sums = own_products(
        chunks, meta, ladder_src, ladder_coef, pair_energy, weights, own, drive[0], eps_row, eps_col
    )
    far_amps, sums = lax.optimization_barrier((far_amps, sums))
    sums = add_products(
        chunks, (1, 2), meta, ladder_src, ladder_coef, weights, (near_amps, far_amps), sums
    )
    outgoing = [far_amps[c.start : c.start + c.length] for c in chunks]
    outgoing[1:], sums = lax.optimization_barrier((outgoing[1:], sums))
    last_amps = [lax.ppermute(x, "occ", NEAR) for x in outgoing[:2]]

    done = []
    for i, chunk in enumerate(chunks):
        parts = (meta, ladder_src, ladder_coef, weights, last_amps[i], sums[i])
        if i < 2:
            away, keep = last_product(chunk, (0, 1), *parts)
        else:
            (away,), (keep,) = [last_product(chunk, (half,), *parts) for half in range(2)]
        if i == 0:
            away[0], outgoing[2] = lax.optimization_barrier((away[0], outgoing[2]))
            last_amps.append(lax.ppermute(outgoing[2], "occ", NEAR))
        if i < 2:
            got = from_other_core(away)
        else:
            got = [lax.ppermute(x, "rep", SWAP) for x in away]
        for_far = keep[0] + got[0]
        if i == 2:
            done[0], for_far = lax.optimization_barrier((done[0], for_far))
        far = lax.ppermute(for_far, "vir", SWAP)
        pieces = (keep[1], got[1], far)
        if i < 2:
            done.append(sum(pieces))
    residual, total = finish(chunks, done, pieces, (rows, width), npair * blocks)
    total = lax.all_to_all(total, ("occ", "vir", "rep"), split_axis=0, concat_axis=0, tiled=True)
    residual, update = jacobi(residual, total, inverse, clip_level * width * math.sqrt(npair))
    return residual[None], update[None]


def any_body(amps, drive, cycle_w, cycle_src, cycle_count, ladder_src, ladder_coef, eps_vir, pair_energy):
    largest_value = lax.Precision.HIGHEST
    pairs_per_unit, rows, width = amps.shape
    nring = cycle_w.shape[1]
    npair = pairs_per_unit * lax.axis_size("occ")
    all_rows = lax.all_gather(amps, "occ", axis=0, tiled=True)
    ladder = jnp.sum(ladder_coef[:, :, None, None] * all_rows[ladder_src], axis=1)
    selected_rows = jnp.take(all_rows, cycle_src.reshape(-1), axis=0).reshape(
        pairs_per_unit, nring, rows, width
    )
    live = (jnp.arange(nring)[None, :] < cycle_count[:, None]).astype(jnp.float32)
    partial_value = jnp.einsum(
        "ptac,ptcb->pab", cycle_w * live[:, :, None, None], selected_rows, precision=largest_value
    )
    cycle = lax.psum_scatter(partial_value, ("vir", "rep"), scatter_dimension=1, tiled=True)
    first_row = lax.axis_index(("vir", "rep")) * rows
    eps_rows = lax.dynamic_slice_in_dim(eps_vir, first_row, rows)
    denom = eps_rows[None, :, None] + eps_vir[None, None, :] - pair_energy[:, None, None]
    residual = drive + cycle + ladder - denom * amps
    total = lax.psum(jnp.sum(residual * residual), ("occ", "vir", "rep"))
    scale = jnp.minimum(1.0, clip_level * width * math.sqrt(npair) / jnp.sqrt(total))
    return residual, scale * residual / denom


def body(*args):
    amps, cycle_w = args[0], args[2]
    pairs_per_unit, rows, width = amps.shape
    chain = (
        pairs_per_unit == 1
        and (lax.axis_size("occ"), lax.axis_size("vir"), lax.axis_size("rep")) == (4, 2, 2)
        and cycle_w.shape[1] >= 4
        and rows % 8 == 0
        and width % LANES == LANES // 4
        and width >= 3 * LANES
    )
    return (chain_body if chain else any_body)(*args)


def solution(mesh):
    in_specs = (
        P(("groups", "occ"), ("vir", "rep"), None),
        P(("groups", "occ"), ("vir", "rep"), None),
        P(("groups", "occ"), None, None, ("vir", "rep")),
        P(("groups", "occ"), None),
        P(("groups", "occ")),
        P(("groups", "occ"), None),
        P(("groups", "occ"), None),
        P("groups"),
        P(("groups", "occ")),
    )
    out_specs = (
        P(("groups", "occ"), ("vir", "rep"), None),
        P(("groups", "occ"), ("vir", "rep"), None),
    )
    return jax.shard_map(body, mesh=mesh, in_specs=in_specs, out_specs=out_specs, check_vma=False)
```

```python
import functools
import math

import jax
import jax.numpy as jnp
from jax import lax
from jax.experimental import pallas as pl
from jax.experimental.pallas import tpu as pltpu
from jax.sharding import PartitionSpec as P

clip_level = 0.5
LANES = 128
SMEM = pl.BlockSpec(memory_space=pltpu.SMEM)
VMEM = pl.BlockSpec(memory_space=pltpu.VMEM)
HBM = pl.BlockSpec(memory_space=pl.ANY)
SWAP = [(0, 1), (1, 0)]
NEAR = [(0, 1), (1, 0), (2, 3), (3, 2)]
FAR = [(0, 2), (2, 0), (1, 3), (3, 1)]
VMEM_MIB = 20


def limit(n):
    return pltpu.CompilerParams(vmem_limit_bytes=n << 20)


class Chunk:
    def __init__(self, rows, width, first, count, rest, start):
        self.rows, self.first, self.count, self.start = rows, first, count, start
        self.rest = width % LANES if rest else 0
        self.at = width - self.rest
        self.group = -(-rows // 32) * 8
        self.length = rows * count + (self.group if self.rest else 0)
        self.width = LANES * count + self.rest

    def take(self, ref):
        parts = [ref[:, self.first * LANES : (self.first + self.count) * LANES]]
        if self.rest:
            parts.append(ref[:, self.at : self.at + self.rest])
        return jnp.concatenate(parts, axis=1) if len(parts) > 1 else parts[0]

    def put(self, ref, value):
        span = LANES * self.count
        ref[:, self.first * LANES : self.first * LANES + span] = value[:, :span]
        if self.rest:
            ref[:, self.at : self.at + self.rest] = value[:, span:]

    def load(self, read):
        parts = [read(t * self.rows, self.rows) for t in range(self.count)]
        if self.rest:
            packed = read(self.count * self.rows, self.group)
            rest = [packed[:, g * self.rest : (g + 1) * self.rest] for g in range(4)]
            parts.append(jnp.concatenate(rest, axis=0)[: self.rows])
        return jnp.concatenate(parts, axis=1)

    def store(self, write, value):
        for t in range(self.count):
            write(t * self.rows, self.rows, value[:, t * LANES : (t + 1) * LANES])
        if self.rest:
            rest = value[:, self.count * LANES :]
            short = 4 * self.group - self.rows
            rest = jnp.concatenate([rest, jnp.zeros((short, self.rest), rest.dtype)], axis=0)
            groups = [rest[g * self.group : (g + 1) * self.group] for g in range(4)]
            write(self.count * self.rows, self.group, jnp.concatenate(groups, axis=1))


def reader(ref, lead=(), skip=0):
    return lambda start, size: ref[(*lead, pl.ds(skip + start, size), slice(None))]


def writer(ref, lead=(), skip=0):
    def write(start, size, value):
        ref[(*lead, pl.ds(skip + start, size), slice(None))] = value

    return write


def split(value):
    high = value.astype(jnp.bfloat16)
    return high, (value - high.astype(jnp.float32)).astype(jnp.bfloat16)


def product(weights, x_high, x_low):
    rows = weights.shape[0] // 2
    dot = functools.partial(jnp.dot, preferred_element_type=jnp.float32)
    value = dot(weights, x_high)
    return value[:rows] + (value[rows:] + dot(weights[:rows], x_low))


def pack(amps, chunks):
    def kernel(amps, out):
        for chunk in chunks:
            chunk.store(writer(out, skip=chunk.start), chunk.take(amps))

    length = sum(chunk.length for chunk in chunks)
    return pl.pallas_call(
        kernel,
        in_specs=[VMEM],
        out_specs=VMEM,
        out_shape=pltpu.VMEM((length, LANES), jnp.float32),
        compiler_params=limit(VMEM_MIB),
        name="pack",
    )(pltpu.with_memory_space_constraint(amps, pltpu.VMEM))


def sum_by_source(meta, cycle_w, cycle_src, cycle_count, npair, blocks):
    nring, depth, height = cycle_w.shape
    rows = height // blocks
    tall, deep = -(-height // LANES) * LANES, -(-depth // LANES) * LANES

    def kernel(meta, src, count, w_ref, out, total, turned, ordered):
        s = pl.program_id(0)

        @pl.when(s == 0)
        def _():
            total[...] = jnp.zeros_like(total)

        @pl.when(s < count[0])
        def _():
            source = src[s]
            total[source, :depth, :height] = total[source, :depth, :height] + w_ref[0]

        @pl.when(s == nring - 1)
        def _():
            for m in range(npair):
                turned[...] = total[m].T
                for j in range(blocks):
                    start = pl.multiple_of(meta[4 + j] * rows, 8)
                    ordered[j * rows : (j + 1) * rows] = turned[pl.ds(start, rows), :depth]
                for h in range(2):
                    high, low = split(ordered[h * height // 2 : (h + 1) * height // 2])
                    out[m, h, : height // 2] = high
                    out[m, h, height // 2 :] = low

    shape = (npair, 2, height, depth)
    return pl.pallas_call(
        kernel,
        grid_spec=pltpu.PrefetchScalarGridSpec(
            num_scalar_prefetch=3,
            grid=(nring,),
            in_specs=[
                pl.BlockSpec(
                    (1, depth, height), lambda s, meta, src, count: (jnp.minimum(s, count[0] - 1), 0, 0)
                )
            ],
            out_specs=pl.BlockSpec(shape, lambda s, *_: (0, 0, 0, 0)),
            scratch_shapes=[
                pltpu.VMEM((npair, deep, tall), jnp.float32),
                pltpu.VMEM((tall, deep), jnp.float32),
                pltpu.VMEM((height, depth), jnp.float32),
            ],
        ),
        out_shape=jax.ShapeDtypeStruct(shape, jnp.bfloat16),
        compiler_params=limit(VMEM_MIB),
        name="sum_by_source",
    )(meta, cycle_src.reshape(-1), cycle_count, cycle_w)


def ladder_weight(source, lad_src, lad_coef):
    weight = jnp.float32(0)
    for entry in range(lad_src.shape[1]):
        weight = weight + jnp.where(lad_src[0, entry] == source, lad_coef[0, entry], 0.0)
    return weight


def own_products(chunks, meta, lad_src, lad_coef, energy, weights, amps, drive, eps_row, eps_col):
    height = weights.shape[2] // 2
    rows = drive.shape[0]

    def kernel(meta, lad_src, lad_coef, energy, weights, amps, drive, eps_row, eps_col, inverse, *outs):
        denom = eps_col[...] + eps_row[...] - energy[0]
        inverse[...] = 1.0 / denom
        weight = ladder_weight(meta[0], lad_src, lad_coef)
        for chunk, out in zip(chunks, outs, strict=True):
            mine = chunk.load(reader(amps, skip=chunk.start))
            x_high, x_low = split(mine)
            for h in range(2):
                out[h] = product(weights[meta[0], h], x_high, x_low)
            denom = eps_col[...] + chunk.take(eps_row) - energy[0]
            base = chunk.take(drive) - denom * mine + weight * mine
            out[1, height - rows :] = out[1, height - rows :] + base

    return pl.pallas_call(
        kernel,
        in_specs=[SMEM] * 4 + [VMEM] * 5,
        out_specs=[VMEM] * (1 + len(chunks)),
        out_shape=[jax.ShapeDtypeStruct(drive.shape, jnp.float32)]
        + [jax.ShapeDtypeStruct((2, height, c.width), jnp.float32) for c in chunks],
        compiler_params=limit(VMEM_MIB),
        name="own_products",
    )(meta, lad_src, lad_coef, energy, weights, amps, drive, eps_row, eps_col)


def add_products(chunks, ks, meta, lad_src, lad_coef, weights, packed, sums):
    height = weights.shape[2] // 2
    rows = chunks[0].rows
    n = len(ks)

    def kernel(meta, lad_src, lad_coef, weights, *refs):
        packed, refs = refs[:n], refs[n:]
        for c, chunk in enumerate(chunks):
            sums, out = refs[c :: len(chunks)]
            amps = [chunk.load(reader(ref, skip=chunk.start)) for ref in packed]
            parts = [split(x) for x in amps]
            for h in range(2):
                value = sums[h]
                for k, (x_high, x_low) in zip(ks, parts, strict=True):
                    value = value + product(weights[meta[k], h], x_high, x_low)
                out[h] = value
            value = out[1, height - rows :]
            for k, x in zip(ks, amps, strict=True):
                value = value + ladder_weight(meta[k], lad_src, lad_coef) * x
            out[1, height - rows :] = value

    return pl.pallas_call(
        kernel,
        in_specs=[SMEM] * 3 + [VMEM] * (1 + n + len(chunks)),
        out_specs=[VMEM] * len(chunks),
        out_shape=[jax.ShapeDtypeStruct(s.shape, jnp.float32) for s in sums],
        compiler_params=limit(VMEM_MIB),
        name="add_products",
    )(meta, lad_src, lad_coef, weights, *packed, *sums)


def last_product(chunk, halves, meta, lad_src, lad_coef, weights, amps, sums):
    npair, height = weights.shape[0], weights.shape[2] // 2
    rows = chunk.rows

    def kernel(meta, lad_src, lad_coef, weights, amps, sums, *outs):
        k = meta[npair - 1]
        x = chunk.load(reader(amps))
        x_high, x_low = split(x)
        for n, half in enumerate(halves):
            value = sums[half] + product(weights[k, half], x_high, x_low)
            for i in range(2):
                part = value[i * rows : (i + 1) * rows]
                if half and i:
                    part = part + ladder_weight(k, lad_src, lad_coef) * x
                chunk.store(writer(outs[2 * n + i]), part)

    outs = pl.pallas_call(
        kernel,
        in_specs=[SMEM] * 3 + [VMEM] * 3,
        out_specs=[VMEM] * (2 * len(halves)),
        out_shape=[jax.ShapeDtypeStruct((chunk.length, LANES), jnp.float32)] * (2 * len(halves)),
        compiler_params=limit(VMEM_MIB),
        name="last_product",
    )(meta, lad_src, lad_coef, weights, amps, sums)
    return [list(outs[2 * n : 2 * n + 2]) for n in range(len(halves))]


def from_other_core(parts):
    n = parts[0].shape[0]
    both = lax.all_gather(jnp.concatenate(parts), "rep", axis=0, tiled=True)
    total = 0.5 * both[: 2 * n] + 0.5 * both[2 * n :]
    return [2.0 * (total[i * n : (i + 1) * n] - 0.5 * part) for i, part in enumerate(parts)]


def finish(chunks, done, pieces, shape, copies):
    def kernel(*refs):
        *refs, out, total_ref = refs
        total = jnp.zeros((1, LANES), jnp.float32)
        for i, chunk in enumerate(chunks):
            parts = refs[i : i + 1] if i < len(done) else refs[len(done) :]
            value = sum(chunk.load(reader(ref)) for ref in parts)
            chunk.put(out, value)
            total = total + jnp.sum(value * value)
        total_ref[...] = jnp.broadcast_to(total, total_ref.shape)

    refs = [*done, *pieces]
    return pl.pallas_call(
        kernel,
        in_specs=[VMEM] * len(refs),
        out_specs=[VMEM, VMEM],
        out_shape=[
            jax.ShapeDtypeStruct(shape, jnp.float32),
            jax.ShapeDtypeStruct((copies, 1, LANES), jnp.float32),
        ],
        compiler_params=limit(VMEM_MIB),
        name="finish",
    )(*refs)


def jacobi(residual, total, inverse, bound):
    rows, width = residual.shape
    part = rows // 5 if rows % 40 == 0 else rows

    def kernel(residual, total, inverse, residual_out, update_out, update, sems):
        copies = [pltpu.make_async_copy(residual, residual_out, sems.at[0])]
        copies[0].start()
        scale = jnp.minimum(1.0, bound / jnp.sqrt(jnp.sum(total[...], axis=0)[0:1, 0:1]))
        for start in range(0, rows, part):
            span = pl.ds(start, part)
            update[span] = (scale * residual[span]) * inverse[span]
            copies.append(pltpu.make_async_copy(update.at[span], update_out.at[span], sems.at[len(copies)]))
            copies[-1].start()
        for copy in copies:
            copy.wait()

    shape = jax.ShapeDtypeStruct(residual.shape, jnp.float32)
    return pl.pallas_call(
        kernel,
        in_specs=[VMEM, VMEM, VMEM],
        out_specs=[HBM, HBM],
        out_shape=[shape, shape],
        scratch_shapes=[
            pltpu.VMEM((rows, width), jnp.float32),
            pltpu.SemaphoreType.DMA((1 + rows // part,)),
        ],
        compiler_params=limit(VMEM_MIB),
        name="jacobi",
    )(residual, total, inverse)


def jacobi(residual, total, inverse, bound):
    def kernel(residual, total, inverse, residual_out, update_out, update, sems):
        whole = pltpu.make_async_copy(residual, residual_out, sems.at[0])
        whole.start()
        scale = jnp.minimum(1.0, bound / jnp.sqrt(jnp.sum(total[...], axis=0)[0:1, 0:1]))
        update[...] = (scale * residual[...]) * inverse[...]
        moved = pltpu.make_async_copy(update, update_out, sems.at[1])
        moved.start()
        whole.wait()
        moved.wait()

    shape = jax.ShapeDtypeStruct(residual.shape, jnp.float32)
    return pl.pallas_call(
        kernel,
        in_specs=[VMEM, VMEM, VMEM],
        out_specs=[HBM, HBM],
        out_shape=[shape, shape],
        scratch_shapes=[pltpu.VMEM(residual.shape, jnp.float32), pltpu.SemaphoreType.DMA((2,))],
        compiler_params=limit(VMEM_MIB),
        name="jacobi",
    )(residual, total, inverse)


def chain_body(amps, drive, cycle_w, cycle_src, cycle_count, ladder_src, ladder_coef, eps_vir, pair_energy):
    _, rows, width = amps.shape
    npair, blocks = lax.axis_size("occ"), width // rows
    place, chip, core = lax.axis_index("occ"), lax.axis_index("vir"), lax.axis_index("rep")
    order = [
        place,
        place ^ 1,
        place ^ 2,
        place ^ 3,
        2 * (1 - chip) + (1 - core),
        2 * chip + (1 - core),
        2 * (1 - chip) + core,
        2 * chip + core,
    ]
    meta = jnp.stack([jnp.asarray(v, jnp.int32) for v in order])
    eps_row = eps_vir.reshape(1, width)
    eps_col = lax.dynamic_slice_in_dim(eps_vir, (2 * chip + core) * rows, rows).reshape(rows, 1)

    chunks, first, start = [], 0, 0
    third = width // LANES // 3
    for count in (third, third, width // LANES - 2 * third):
        chunks.append(Chunk(rows, width, first, count, first + count == width // LANES, start))
        first, start = first + count, start + chunks[-1].length
    own = pack(amps[0], chunks)
    far_amps = lax.ppermute(own, "occ", FAR)
    near_amps = lax.ppermute(own, "occ", NEAR)
    weights = sum_by_source(meta, jnp.swapaxes(cycle_w[0], 1, 2), cycle_src, cycle_count, npair, blocks)
    inverse, *sums = own_products(
        chunks, meta, ladder_src, ladder_coef, pair_energy, weights, own, drive[0], eps_row, eps_col
    )
    far_amps, sums = lax.optimization_barrier((far_amps, sums))
    sums = add_products(
        chunks, (1, 2), meta, ladder_src, ladder_coef, weights, (near_amps, far_amps), sums
    )
    outgoing = [far_amps[c.start : c.start + c.length] for c in chunks]
    outgoing[1:], sums = lax.optimization_barrier((outgoing[1:], sums))
    last_amps = [lax.ppermute(x, "occ", NEAR) for x in outgoing]

    done = []
    for i, chunk in enumerate(chunks):
        parts = (meta, ladder_src, ladder_coef, weights, last_amps[i], sums[i])
        if i < 2:
            away, keep = last_product(chunk, (0, 1), *parts)
        else:
            (away,), (keep,) = [last_product(chunk, (half,), *parts) for half in range(2)]
        if i < 2:
            got = from_other_core(away)
        else:
            got = [lax.ppermute(x, "rep", SWAP) for x in away]
        for_far = keep[0] + got[0]
        if i == 2:
            done[0], for_far = lax.optimization_barrier((done[0], for_far))
        far = lax.ppermute(for_far, "vir", SWAP)
        pieces = (keep[1], got[1], far)
        if i < 2:
            done.append(sum(pieces))
    residual, total = finish(chunks, done, pieces, (rows, width), npair * blocks)
    total = lax.all_to_all(total, ("occ", "vir", "rep"), split_axis=0, concat_axis=0, tiled=True)
    residual, update = jacobi(residual, total, inverse, clip_level * width * math.sqrt(npair))
    return residual[None], update[None]


def any_body(amps, drive, cycle_w, cycle_src, cycle_count, ladder_src, ladder_coef, eps_vir, pair_energy):
    largest_value = lax.Precision.HIGHEST
    pairs_per_unit, rows, width = amps.shape
    nring = cycle_w.shape[1]
    npair = pairs_per_unit * lax.axis_size("occ")
    all_rows = lax.all_gather(amps, "occ", axis=0, tiled=True)
    ladder = jnp.sum(ladder_coef[:, :, None, None] * all_rows[ladder_src], axis=1)
    selected_rows = jnp.take(all_rows, cycle_src.reshape(-1), axis=0).reshape(
        pairs_per_unit, nring, rows, width
    )
    live = (jnp.arange(nring)[None, :] < cycle_count[:, None]).astype(jnp.float32)
    partial_value = jnp.einsum(
        "ptac,ptcb->pab", cycle_w * live[:, :, None, None], selected_rows, precision=largest_value
    )
    cycle = lax.psum_scatter(partial_value, ("vir", "rep"), scatter_dimension=1, tiled=True)
    first_row = lax.axis_index(("vir", "rep")) * rows
    eps_rows = lax.dynamic_slice_in_dim(eps_vir, first_row, rows)
    denom = eps_rows[None, :, None] + eps_vir[None, None, :] - pair_energy[:, None, None]
    residual = drive + cycle + ladder - denom * amps
    total = lax.psum(jnp.sum(residual * residual), ("occ", "vir", "rep"))
    scale = jnp.minimum(1.0, clip_level * width * math.sqrt(npair) / jnp.sqrt(total))
    return residual, scale * residual / denom


def body(*args):
    amps, cycle_w = args[0], args[2]
    pairs_per_unit, rows, width = amps.shape
    chain = (
        pairs_per_unit == 1
        and (lax.axis_size("occ"), lax.axis_size("vir"), lax.axis_size("rep")) == (4, 2, 2)
        and cycle_w.shape[1] >= 4
        and rows % 8 == 0
        and width % LANES == LANES // 4
        and width >= 3 * LANES
    )
    return (chain_body if chain else any_body)(*args)


def solution(mesh):
    in_specs = (
        P(("groups", "occ"), ("vir", "rep"), None),
        P(("groups", "occ"), ("vir", "rep"), None),
        P(("groups", "occ"), None, None, ("vir", "rep")),
        P(("groups", "occ"), None),
        P(("groups", "occ")),
        P(("groups", "occ"), None),
        P(("groups", "occ"), None),
        P("groups"),
        P(("groups", "occ")),
    )
    out_specs = (
        P(("groups", "occ"), ("vir", "rep"), None),
        P(("groups", "occ"), ("vir", "rep"), None),
    )
    return jax.shard_map(body, mesh=mesh, in_specs=in_specs, out_specs=out_specs, check_vma=False)
```
